32 devices in a mesh: dp: 8 (over z, y), head: 4 (over x, core).
Axes of the slice: x: 2, y: 2, z: 4, core: 2. Of those that a mesh axis runs over, the one named last changes fastest.
Arguments:
- hidden: bfloat16 [8, 1088, 1024], P('dp', 'head'), may hold values from -6 to 6
- memory: bfloat16 [8, 1088, 1024], P('dp', 'head'), may hold values from -6 to 6
- out_grad: bfloat16 [8, 1088, 1024], P('dp', 'head'), may hold values from -6 to 6
- valid_mask: int32 [8, 1088], P('dp', 'head'), may hold values from 0 to 1, as said below
- memory_length: int32 [8], P('dp'), may hold values from 545 to 1088, as said below
- value_routes: int32 [8, 2, 1088, 4, 2], P('dp', None, 'head'), may hold values from 0 to 4, all different within a row
- out_routes: int32 [8, 1088, 4, 2], P('dp', 'head'), may hold values from 0 to 4, all different within a row
- norm_gain: float32 [2, 1024], replicated, may hold values from 0.5 to 1.5
- norm_bias: float32 [2, 1024], replicated, may hold values from -1 to 1
- query_weight: bfloat16 [1024, 448], P('dp', 'head'), may hold values from -0.1875 to 0.1875
- key_weight: bfloat16 [1024, 448], P('dp', 'head'), may hold values from -0.25 to 0.25
- rel_weight: bfloat16 [1024, 448], P('dp', 'head'), may hold values from -0.25 to 0.25
- value_weight: bfloat16 [1024, 2240], P('dp', 'head'), may hold values from -0.1875 to 0.1875
- value_router: bfloat16 [1024, 20], P('dp', 'head'), may hold values from -0.125 to 0.125
- out_router: bfloat16 [1024, 20], P('dp', 'head'), may hold values from -0.125 to 0.125
- out_weight: bfloat16 [2240, 1024], P('head', 'dp'), may hold values from -6 to 6
- position_bias: float32 [2, 448], P(None, 'head'), may hold values from -3 to 3
- up_weight: bfloat16 [4096, 1024], P(('dp', 'head')), may hold values from -0.1875 to 0.1875
- down_weight: bfloat16 [4096, 1024], P(('dp', 'head')), may hold values from -0.125 to 0.125
Outputs:
- out_hidden: bfloat16 [8, 1088, 1024], P('dp', 'head')
- in_grad: float32 [8, 1088, 1024], P('dp', 'head')
- norm_gain_grad: float32 [2, 1024], replicated
- norm_bias_grad: float32 [2, 1024], replicated
- query_grad: float32 [1024, 448], P('dp', 'head')
- key_grad: float32 [1024, 448], P('dp', 'head')
- rel_grad: float32 [1024, 448], P('dp', 'head')
- value_grad: float32 [1024, 2240], P('dp', 'head')
- value_router_grad: float32 [1024, 20], P('dp', 'head')
- out_router_grad: float32 [1024, 20], P('dp', 'head')
- out_weight_grad: float32 [2240, 1024], P('head', 'dp')
- position_bias_grad: float32 [2, 448], replicated
- up_grad: float32 [4096, 1024], P(('dp', 'head'))
- down_grad: float32 [4096, 1024], P(('dp', 'head'))
- layer_stats: float32 [2], replicated
The draws below stay inside these ranges and needn't reach their ends.
Inputs may be any that keep to these rules, and one draw needn't show every extreme that they name: In each sequence the tokens with valid_mask = 1 form a prefix of more than 816 tokens, and some sequence is valid throughout. `memory_length`: some sequence has all 1088 memory slots valid, and every sequence more than half of them. `value_routes`: the 2 experts named for one token and head differ. `out_routes`: the 2 experts named for one token and head differ.
All inputs are finite; a program needn't handle non-finite values.
Results may differ from the reference program's by a relative error of at most 0.02.
Values may be sent and summed in bfloat16 or wider, within the bound.
No kernel may reach another device: no remote copies, remote signals or barrier semaphores. Data moves between devices by JAX's collectives and lax.ppermute only.
A program may use at most 256 MiB of HBM per device.

```python
import math
import jax
import jax.numpy as jnp
from jax import lax

D = 1024
HEADS = 4
DH = 112
EXPERTS = 5
TOPK = 2
FF = 4096
QB = 544
LEN = 1088
MEM = 1088
KEYS = 2176
SEQS = 8


def draw_valid_mask(key, part):
    key = jax.random.fold_in(key, 3)
    cuts = jax.random.randint(key, (SEQS,), 0, LEN // 4)
    chosen = jax.random.randint(jax.random.fold_in(key, 1), (), 0, SEQS)
    cuts = jnp.where(jnp.arange(SEQS) == chosen, 0, cuts)
    return (jnp.arange(LEN)[None, :] < (LEN - cuts)[:, None]).astype(jnp.int32)


def draw_memory_length(key, part):
    key = jax.random.fold_in(key, 5)
    cuts = jax.random.randint(key, (SEQS,), 0, MEM // 2)
    chosen = jax.random.randint(jax.random.fold_in(key, 1), (), 0, SEQS)
    cuts = jnp.where(jnp.arange(SEQS) == chosen, 0, cuts)
    return (MEM - cuts).astype(jnp.int32)


def block_levels(own_key, extent, split, smallest, largest):
    loudness = 1.0
    for axis_at, shards_of in split:
        heights = jax.random.uniform(jax.random.fold_in(jax.random.fold_in(own_key, 6), axis_at), (shards_of,), jnp.float32, smallest / len(split), largest / len(split))
        loudness = loudness * jnp.repeat(jnp.exp(heights), extent[axis_at] // shards_of).reshape((-1,) + (1,) * (len(extent) - 1 - axis_at))
    return loudness


def different_ones(stream_key, rows, number_of, top, lift):
    sequence = jax.random.permutation(jax.random.fold_in(stream_key, 1), number_of)
    pull = sequence
    for power in range(3):
        pull = pull * pull // number_of
    pull = pull * lift // number_of
    chance = jax.random.randint(jax.random.fold_in(stream_key, 2), (rows, number_of), 0, 4096) + pull
    holders = jax.random.permutation(jax.random.fold_in(stream_key, 3), rows)[jnp.arange(number_of) % rows]
    chance = jnp.where(jnp.arange(rows)[:, None] == holders[None, :], 1 << 14, chance)
    score = chance * number_of + jnp.arange(number_of)
    return lax.top_k(score.astype(jnp.int32), top)[1].astype(jnp.int32)


def bell_draw(key, dims, scale, most, split=(), dtype=jnp.bfloat16):
    values = scale * jax.random.normal(key, dims, jnp.float32)
    if split:
        values = values * block_levels(key, dims, split, -0.22, 0.18)
    return jnp.clip(values, -most, most).astype(dtype)


def setup_inputs(seed: int = 0) -> dict:
    seeds = jax.random.split(jax.random.key(seed), 20)
    return {
        "hidden": bell_draw(seeds[0], (SEQS, LEN, D), 1.0, 6.0, ((0, 8), (1, 4))),
        "memory": bell_draw(seeds[1], (SEQS, MEM, D), 1.0, 6.0, ((0, 8), (1, 4))),
        "out_grad": bell_draw(seeds[2], (SEQS, LEN, D), 1.0, 6.0, ((0, 8), (1, 4))),
        "valid_mask": draw_valid_mask(jax.random.fold_in(seeds[19], 71), 0),
        "memory_length": draw_memory_length(jax.random.fold_in(seeds[19], 71), 0),
        "value_routes": different_ones(seeds[5], SEQS * 2 * LEN * HEADS, EXPERTS, TOPK, 6553).reshape((SEQS, 2, LEN, HEADS, TOPK)),
        "out_routes": different_ones(seeds[6], SEQS * LEN * HEADS, EXPERTS, TOPK, 6553).reshape((SEQS, LEN, HEADS, TOPK)),
        "norm_gain": jnp.clip(1.0 + 0.1 * jax.random.normal(seeds[7], (2, D), jnp.float32), 0.5, 1.5),
        "norm_bias": bell_draw(seeds[8], (2, D), 0.2, 1.0, (), jnp.float32),
        "query_weight": bell_draw(seeds[9], (D, HEADS * DH), D ** -0.5, 0.1875, ((0, 8), (1, 4))),
        "key_weight": bell_draw(seeds[10], (D, HEADS * DH), (D // 2) ** -0.5, 0.25, ((0, 8), (1, 4))),
        "rel_weight": bell_draw(seeds[11], (D, HEADS * DH), (D // 2) ** -0.5, 0.25, ((0, 8), (1, 4))),
        "value_weight": bell_draw(seeds[12], (D, HEADS * EXPERTS * DH), D ** -0.5, 0.1875, ((0, 8), (1, 4))),
        "value_router": bell_draw(seeds[13], (D, HEADS * EXPERTS), (2 * D) ** -0.5, 0.125, ((0, 8), (1, 4))),
        "out_router": bell_draw(seeds[14], (D, HEADS * EXPERTS), (2 * D) ** -0.5, 0.125, ((0, 8), (1, 4))),
        "out_weight": bell_draw(seeds[15], (HEADS * EXPERTS * DH, D), 1 ** -0.5, 6.0, ((0, 4), (1, 8))),
        "position_bias": bell_draw(seeds[16], (2, HEADS * DH), 0.5, 3.0, ((1, 4),), jnp.float32),
        "up_weight": bell_draw(seeds[17], (FF, D), D ** -0.5, 0.1875, ((0, 32),)),
        "down_weight": bell_draw(seeds[18], (FF, D), (FF // 2) ** -0.5, 0.125, ((0, 32),)),
    }


@jax.custom_vjp
def low(v):
    return lax.optimization_barrier(v.astype(jnp.bfloat16)).astype(jnp.float32)

@jax.custom_vjp
def low_back(v):
    return v

def low_keep(v):
    return (low(v), None)

def low_pass(kept, grad):
    return (grad,)

def back_keep(v):
    return (v, None)

def back_low(kept, grad):
    return (low(grad),)
low.defvjp(low_keep, low_pass)
low_back.defvjp(back_keep, back_low)
highest = lax.Precision.HIGHEST
epsilon = 1e-05
negative = -1e+30

def matmul(left, right):
    return jnp.dot(left, right, precision=highest, preferred_element_type=jnp.float32)

def layer_norm(source, gain, bias):
    center = source - lax.optimization_barrier(jnp.mean(source, axis=-1, keepdims=True))
    inverse = lax.rsqrt(lax.optimization_barrier(jnp.mean(center * center, axis=-1, keepdims=True)) + epsilon)
    return center * inverse * gain + bias

def sinusoid(length, model_width):
    places = jnp.arange(length).astype(jnp.float32)
    frequency = jnp.exp(jnp.arange(0, model_width, 2).astype(jnp.float32) * (-math.log(10000.0) / model_width))
    angles = places[:, None] * frequency[None, :]
    return jnp.concatenate([jnp.sin(angles), jnp.cos(angles)], axis=1)

def shift_rows(matrix, key_count):
    row_count, width_in = matrix.shape
    flat = matrix.reshape(-1)[row_count - 1:row_count - 1 + row_count * (width_in - 1)]
    return flat.reshape(row_count, width_in - 1)[:, :key_count]

def selection(routes):
    experts = jnp.arange(EXPERTS).astype(jnp.int32)
    return lax.optimization_barrier(jnp.sum((routes[..., None] == experts).astype(jnp.float32), axis=-2))

def one_head(head_pack, normed, joined, sin_table, key_valid):
    query_w, key_w, rel_w, value_w, value_gate_w, out_gate_w, out_w, bias_content, bias_position, value_pick, out_pick = head_pack
    score_scale = 1.0 / math.sqrt(DH)
    queries = low_back(matmul(normed, query_w))
    content_query = low(queries + bias_content)
    position_query = low(queries + bias_position)
    key_rows = low(low_back(matmul(joined, key_w)))
    expert_in = low_back(matmul(joined, value_w))
    value_gate = jax.nn.sigmoid(low_back(matmul(joined, value_gate_w))) * value_pick
    values = low(lax.optimization_barrier(jnp.sum(value_gate[:, :, None] * expert_in.reshape(KEYS, EXPERTS, DH), axis=1)))
    rel_rows = low(low_back(matmul(sin_table, rel_w)))
    rel_desc = jnp.concatenate([rel_rows[::-1], jnp.zeros((KEYS - 1, DH), jnp.float32)], axis=0)

    def block(offset):
        qu_block = lax.dynamic_slice_in_dim(content_query, offset, QB)
        qv_block = lax.dynamic_slice_in_dim(position_query, offset, QB)
        window = lax.dynamic_slice_in_dim(rel_desc, LEN - QB - offset, KEYS + QB - 1)
        content = matmul(qu_block, key_rows.T)
        position = shift_rows(matmul(qv_block, window.T), KEYS)
        scores = low_back((content + position) * score_scale)
        positions = offset + jnp.arange(QB).astype(jnp.int32)
        allowed = key_valid[None, :] & (jnp.arange(KEYS).astype(jnp.int32)[None, :] <= MEM + positions[:, None])
        scores = jnp.where(allowed, scores, negative)
        row_max = lax.optimization_barrier(jnp.max(scores, axis=1, keepdims=True))
        weights_exp = jnp.exp(scores - row_max)
        softmax_rows = low(weights_exp / lax.optimization_barrier(jnp.sum(weights_exp, axis=1, keepdims=True)))
        return matmul(softmax_rows, values)
    offsets = jnp.arange(LEN // QB).astype(jnp.int32) * QB
    attended = low_back(lax.map(jax.checkpoint(block), offsets).reshape(LEN, DH))
    out_gate = jax.nn.sigmoid(low_back(matmul(normed, out_gate_w))) * out_pick
    mixture = low((out_gate[:, :, None] * attended[:, None, :]).reshape(LEN, EXPERTS * DH))
    return low(matmul(mixture, out_w))

def layer(rows_in, norm_gain, norm_bias, query_weight, key_weight, rel_weight, value_weight, value_router, out_router, out_weight, position_bias, up_weight, down_weight, memory_rows, sin_table, key_valid, value_pick, out_pick):
    normed = low(layer_norm(rows_in, norm_gain[0], norm_bias[0]))
    normed_memory = low(layer_norm(memory_rows, norm_gain[0], norm_bias[0]))
    joined = jnp.concatenate([normed_memory, normed], axis=0)
    head_packs = (query_weight.reshape(D, HEADS, DH).transpose(1, 0, 2), key_weight.reshape(D, HEADS, DH).transpose(1, 0, 2), rel_weight.reshape(D, HEADS, DH).transpose(1, 0, 2), value_weight.reshape(D, HEADS, EXPERTS * DH).transpose(1, 0, 2), value_router.reshape(D, HEADS, EXPERTS).transpose(1, 0, 2), out_router.reshape(D, HEADS, EXPERTS).transpose(1, 0, 2), out_weight.reshape(HEADS, EXPERTS * DH, D), position_bias[0].reshape(HEADS, DH), position_bias[1].reshape(HEADS, DH), value_pick.transpose(1, 0, 2), out_pick.transpose(1, 0, 2))
    head_outs = lax.map(lambda head_pack: one_head(head_pack, normed, joined, sin_table, key_valid), head_packs)
    branch = low_back(lax.optimization_barrier(jnp.sum(head_outs, axis=0)))
    middle = rows_in + branch
    normed_two = low(layer_norm(middle, norm_gain[1], norm_bias[1]))
    pre_act = low_back(matmul(normed_two, up_weight.T))
    inner = low(jax.nn.gelu(pre_act, approximate=False))
    return (middle + matmul(inner, down_weight), branch)

def reference(hidden, memory, out_grad, valid_mask, memory_length, value_routes, out_routes, norm_gain, norm_bias, query_weight, key_weight, rel_weight, value_weight, value_router, out_router, out_weight, position_bias, up_weight, down_weight):
    sin_table = low(sinusoid(KEYS, D))
    params = tuple((param.astype(jnp.float32) for param in (norm_gain, norm_bias, query_weight, key_weight, rel_weight, value_weight, value_router, out_router, out_weight, position_bias, up_weight, down_weight)))

    def one_sequence(carry, item):
        rows_in, memory_rows, grad_rows, valid_row, memory_count, value_route, out_route = item
        key_valid = jnp.concatenate([jnp.arange(MEM).astype(jnp.int32) >= MEM - memory_count, valid_row > 0])
        value_pick = selection(jnp.concatenate([value_route[0], value_route[1]], axis=0))
        out_pick = selection(out_route)

        def forward(*inputs):
            return layer(*inputs, memory_rows, sin_table, key_valid, value_pick, out_pick)
        result, pullback, branch = jax.vjp(forward, rows_in, *params, has_aux=True)
        grads = pullback(grad_rows)
        marks = valid_row.astype(jnp.float32)[:, None]
        sums = jnp.stack([jnp.sum(marks * result * result), jnp.sum(marks * branch * branch), jnp.sum(marks)])
        updated = tuple((total + extra for total, extra in zip(carry, tuple(grads[1:]) + (sums,))))
        return (updated, (result.astype(jnp.bfloat16), grads[0]))
    start_totals = tuple((jnp.zeros_like(param) for param in params)) + (jnp.zeros((3,), jnp.float32),)
    items = (hidden.astype(jnp.float32), memory.astype(jnp.float32), out_grad.astype(jnp.float32), valid_mask, memory_length, value_routes, out_routes)
    totals, (results, in_grads) = lax.scan(one_sequence, start_totals, items)
    sums = totals[12]
    layer_stats = jnp.sqrt(sums[:2] / (D * sums[2]))
    return (results, in_grads, totals[0], totals[1], totals[2], totals[3], totals[4], totals[5], totals[6], totals[7], totals[8], totals[9], totals[10], totals[11], layer_stats)
```

```python
import math

import jax
import jax.numpy as jnp
import numpy as np
from jax import lax
from jax.experimental import pallas as pl
from jax.experimental.pallas import tpu as pltpu
from jax.sharding import PartitionSpec as P

EXPERTS = 5
LANES = 128
NEG = -1e30
EPS = 1e-05
BF = jnp.bfloat16
F32 = jnp.float32
RING = 8
SPREAD = EXPERTS * LANES
KEYVAL = LANES + SPREAD
FIRST = 2 * LANES + SPREAD + LANES


def mm(left, right):
    return jnp.dot(left, right, preferred_element_type=F32)


def mm_tn(left, right):
    return lax.dot_general(left, right, (((0,), (0,)), ((), ())), preferred_element_type=F32)


def mm_nt(left, right):
    return lax.dot_general(left, right, (((1,), (1,)), ((), ())), preferred_element_type=F32)


def hold(*values):
    return lax.optimization_barrier(values)


def shape(dims, dtype=BF):
    return jax.ShapeDtypeStruct(tuple(dims), dtype)


def padded_bytes(item):
    dims = list(item.shape)
    size = jnp.dtype(item.dtype).itemsize
    dims[-1] = -(-dims[-1] // LANES) * LANES
    if len(dims) > 1:
        dims[-2] = -(-dims[-2] // 16) * 16
    return size * math.prod(dims)


def kernel_call(body, outs, name, flops, scratch=(), scalars=0, spare=7, hbm=(), copies=0):
    def call(*operands):
        smem = pl.BlockSpec(memory_space=pltpu.SMEM)
        vmem = pl.BlockSpec(memory_space=pltpu.VMEM)
        far = pl.BlockSpec(memory_space=pltpu.HBM)
        total = sum(padded_bytes(item) for item in scratch)
        spaces = [pltpu.VMEM(x.shape, x.dtype) for x in scratch]
        if copies:
            spaces.append(pltpu.SemaphoreType.DMA((copies,)))
        return pl.pallas_call(
            body,
            out_shape=tuple(outs),
            in_specs=[
                smem if i < scalars else far if i in hbm else vmem for i in range(len(operands))
            ],
            out_specs=tuple(vmem for _ in outs),
            scratch_shapes=spaces,
            compiler_params=pltpu.CompilerParams(vmem_limit_bytes=total + (spare << 20)),
            cost_estimate=pl.CostEstimate(
                flops=int(flops) // 16, bytes_accessed=1 << 10, transcendentals=0
            ),
            name=name,
        )(*operands)

    return call


def flip(value, bit):
    count = lax.axis_size("head")
    return lax.ppermute(value, "head", [(i, i ^ bit) for i in range(count)])


def ring_order(count):
    return list(range(0, count, 2)) + list(range(count - 1, 0, -2))


def ring_place():
    index = lax.axis_index("dp")
    count = lax.axis_size("dp")
    return jnp.where(index & 1 == 0, index >> 1, count - 1 - (index >> 1)).astype(jnp.int32)


def ring_index(info_ref, offset):
    place = lax.rem(info_ref[1] + offset, RING)
    return jnp.where(place < RING // 2, 2 * place, 2 * RING - 1 - 2 * place)


def step(value, direction):
    count = lax.axis_size("dp")
    order = ring_order(count)
    return lax.ppermute(
        value, "dp", [(order[i], order[(i + direction) % count]) for i in range(count)]
    )


def tile_half(rows):
    return -(-(rows // 2) // 16) * 16


class RingGather:
    def __init__(self, own, axis):
        self.ring = lax.axis_size("dp") == RING
        self.half = tile_half(own.shape[0])
        self.round = 0
        if self.ring:
            self.blocks = [own]
            self.pieces = [(0, 0)]
            self.right, self.left = own, own
        else:
            self.blocks = [lax.all_gather(own, "dp", axis=axis, tiled=True)]
            self.pieces = [(0, 0)]

    def advance(self):
        if not self.ring or self.round == RING // 2:
            return
        self.round += 1
        k, half = self.round, self.half
        if k < RING // 2:
            self.right, self.left = step(self.right, 1), step(self.left, -1)
            self.pieces += [(RING - k, 0), (k, 0)]
        else:
            self.right, self.left = step(self.right[:half], 1), step(self.left[half:], -1)
            self.pieces += [(k, 0), (k, half)]
        self.blocks += [self.right, self.left]

    def arrived(self, *values):
        if not self.ring:
            return values
        out = hold(*values, self.right, self.left)
        self.right, self.left = out[-2:]
        self.blocks[-2:] = [self.right, self.left]
        return out[:-2]

    def arrived_last(self, *values):
        if not self.ring:
            return values
        return hold(*values, *self.blocks[-2:])[:-2]


def ring_add(ahead, right, behind, left):
    count = len(ahead)
    heights = [block.shape[0] for block in ahead]
    total = sum(heights)
    width = ahead[0].shape[1]

    def lay(out_ref, refs, got_ref, start):
        stop = start + got_ref.shape[0]
        first = 0
        for ref, rows in zip(refs, heights):
            low, high = max(start, first), min(stop, first + rows)
            if low < high:
                value = ref[low - first : high - first, :].astype(F32)
                value = value + got_ref[low - start : high - start, :].astype(F32)
                out_ref[low:high, :] = value.astype(BF)
            for begin, end in ((first, min(start, first + rows)), (max(stop, first), first + rows)):
                if begin < end:
                    out_ref[begin:end, :] = ref[begin - first : end - first, :]
            first += rows

    def body(*refs):
        a_refs, r_ref = refs[:count], refs[count]
        b_refs, l_ref = refs[count + 1 : 2 * count + 1], refs[2 * count + 1]
        ahead_ref, behind_ref = refs[2 * count + 2 :]
        lay(ahead_ref, a_refs, r_ref, 0)
        lay(behind_ref, b_refs, l_ref, total - left.shape[0])

    return kernel_call(
        body, [shape((total, width))] * 2, "ring_add", 8 * total * width
    )(*ahead, right, *behind, left)


class RingSum:
    def __init__(self, groups, upper, lower, axis):
        self.groups = groups
        self.axis = axis
        self.ring = lax.axis_size("dp") == RING
        self.rest = 0
        if self.ring:
            self.rest = RING // 2 - 1
            self.right, self.left = step(upper, 1), step(lower, -1)

    def advance(self):
        if not self.rest:
            return
        k = self.rest
        ahead, behind = ring_add(
            [blocks[k] for blocks in self.groups],
            self.right,
            [blocks[RING - k] for blocks in self.groups],
            self.left,
        )
        self.right, self.left = step(ahead, 1), step(behind, -1)
        self.rest -= 1

    def arrived(self, *values):
        if not self.ring:
            return values
        out = hold(*values, self.right, self.left)
        self.right, self.left = out[-2:]
        return out[:-2]

    def finish(self, outs, name):
        count = len(self.groups)
        if self.ring:
            while self.rest:
                self.advance()
            parts = [blocks[0] for blocks in self.groups] + [self.right, self.left]
        else:
            parts = [
                lax.psum_scatter(blocks[0], "dp", scatter_dimension=self.axis, tiled=True)
                for blocks in self.groups
            ]
        starts = [0]
        for part in parts[: count - 1]:
            starts.append(starts[-1] + part.shape[0])

        def body(*refs):
            ins, results = refs[: len(parts)], refs[len(parts) :]
            for result, (which, row, rows, column, columns) in zip(results, outs):
                across = slice(column, column + columns)
                total = ins[which][row : row + rows, across].astype(F32)
                first = starts[which] + row
                for ref in ins[count:]:
                    total = total + ref[first : first + rows, across].astype(F32)
                result[...] = total

        shapes = [shape((cuts[2], cuts[4]), F32) for cuts in outs]
        return kernel_call(body, shapes, name, 8 * parts[0].size)(*parts)


def sum_over_dp(value, bit):
    count = lax.axis_size("dp")
    return value + lax.ppermute(value, "dp", [(i, i ^ bit) for i in range(count)])


def packed_rows(head_width):
    inside = EXPERTS * head_width
    items = [(0, 0, LANES), (LANES, LANES, LANES)]
    for e in range(EXPERTS):
        items.append((2 * LANES + e * head_width, (2 + e) * LANES, head_width))
    items.append((2 * LANES + inside, LANES + KEYVAL, head_width))
    for e in range(EXPERTS):
        items.append((2 * LANES + inside + (1 + e) * head_width, FIRST + e * LANES, head_width))
    return items


def lay_columns(whole, refs, pieces, info_ref, head_width):
    total = whole.shape[1]
    items = packed_rows(head_width)
    for _, target, rows in items:
        if rows < LANES:
            whole[target + rows : target + LANES, :] = jnp.zeros((LANES - rows, total), BF)
    for ref, (offset, start) in zip(refs, pieces):
        height, width = ref.shape
        for source, target, rows in items:
            low, high = max(source, start), min(source + rows, start + height)
            if low >= high:
                continue
            value = ref[low - start : high - start, :]
            there = slice(target + low - source, target + high - source)
            if width == total:
                whole[there, :] = value
            else:
                column = pl.multiple_of(ring_index(info_ref, offset) * width, LANES)
                whole[there, pl.ds(column, width)] = value


def norm_rows(source, gain, bias):
    center = source - jnp.mean(source, axis=-1, keepdims=True)
    inverse = lax.rsqrt(jnp.mean(center * center, axis=-1, keepdims=True) + EPS)
    unit = center * inverse
    return unit, inverse, unit * gain + bias


def pack_weights(info, query, out_router, key, value_router, value, rel, out_weight, memory, hidden):
    part = query.shape[1]
    head_width = query.shape[0]
    tail = LANES - head_width

    own, width = hidden.shape

    def body(
        info_ref, q_ref, or_ref, k_ref, vr_ref, v_ref, r_ref, o_ref, m_ref, h_ref, out_ref, rows_ref, routers, sems
    ):
        moves = [(or_ref, routers.at[0]), (vr_ref, routers.at[1])]
        first = 2 * LANES
        for ref in (v_ref, r_ref, o_ref):
            moves.append((ref, out_ref.at[first : first + ref.shape[0], :]))
            first += ref.shape[0]
        for ref, first in ((q_ref, 0), (k_ref, LANES)):
            moves.append((ref, out_ref.at[first : first + head_width, :]))
        moves += [(m_ref, rows_ref.at[0:own, :]), (h_ref, rows_ref.at[own : 2 * own, :])]
        started = []
        for index, (source, target) in enumerate(moves):
            copy = pltpu.make_async_copy(source, target, sems.at[index])
            copy.start()
            started.append(copy)
        started[0].wait()
        started[1].wait()
        for index in range(2):
            rest = jnp.concatenate(
                [routers[index].astype(F32), jnp.zeros((tail - EXPERTS, part), F32)], axis=0
            )
            first = LANES * index + head_width
            out_ref[first : first + tail, :] = rest.astype(BF)
        for copy in started[2:]:
            copy.wait()

    return kernel_call(
        body,
        [shape((2 * LANES + (2 * EXPERTS + 1) * head_width, part)), shape((2 * own, width))],
        "pack_weights",
        1 << 20,
        scratch=[shape((2, EXPERTS, part))],
        scalars=1,
        spare=54,
        hbm=tuple(range(1, 10)),
        copies=9,
    )(info, query, out_router, key, value_router, value, rel, out_weight, memory, hidden)


def first_norm(parts, gain, bias, name):
    rows, width = parts[0].shape
    count = len(parts)

    def body(*refs):
        gain_ref, bias_ref, out_ref = refs[count:]
        for k in range(count):
            source = refs[k][...].astype(F32)
            out_ref[k] = norm_rows(source, gain_ref[0:1, :], bias_ref[0:1, :])[2].astype(BF)

    return kernel_call(
        body, [shape((count, rows, width))], name, count * 400 * rows * width
    )(*parts, gain, bias)[0]


def route_codes(value_routes, out_routes, valid_mask):
    heads, _, own = out_routes.shape
    lines = 6 * heads + 1
    total = -(-lines // 16) * 16

    def body(v_ref, o_ref, m_ref, out_ref):
        parts = [v_ref[kind, head].astype(F32) for kind in range(2) for head in range(heads)]
        parts += [o_ref[head].astype(F32) for head in range(heads)]
        parts += [m_ref[...].astype(F32), jnp.zeros((total - lines, own), F32)]
        out_ref[...] = jnp.concatenate(parts, axis=0).astype(BF)

    return kernel_call(body, [shape((total, own))], "route_codes", 1 << 16)(
        value_routes, out_routes, valid_mask
    )[0]


def route_lanes(info, codes, heads, head_width):
    lines, own = codes[0].shape
    rows = own * heads

    def body(info_ref, c0, c1, c2, c3, pick_v_ref, pick_o_ref):
        row = lax.broadcasted_iota(jnp.int32, (own, own), 0)
        same = jnp.where(row == lax.broadcasted_iota(jnp.int32, (own, own), 1), 1.0, 0.0).astype(BF)
        expert = lax.broadcasted_iota(jnp.int32, (LANES, own), 0) - head_width
        expert = expert.astype(F32)
        last = lax.broadcasted_iota(jnp.int32, (LANES, own), 0) == LANES - 1
        for k, ref in enumerate((c0, c1, c2, c3)):
            lines_all = ref[...].astype(F32)
            place = (info_ref[0] ^ k) * own
            for kind in range(3):
                named = []
                for choice in range(2):
                    line = jnp.zeros((1, own), F32)
                    for head in range(heads):
                        at = (kind * heads + head) * 2 + choice
                        line = line + jnp.where(
                            info_ref[0] == head, lines_all[at : at + 1, :], 0.0
                        )
                    named.append(line)
                hit = (expert == named[0]) | (expert == named[1])
                lanes = jnp.where(hit, 1.0, 0.0)
                if kind == 1:
                    lanes = jnp.where(last, lines_all[6 * heads : 6 * heads + 1, :], lanes)
                picked = mm_nt(same, lanes.astype(BF)).astype(BF)
                if kind == 2:
                    pick_o_ref[pl.ds(pl.multiple_of(place, 16), own), :] = picked
                else:
                    start = pl.multiple_of(place + kind * rows, 16)
                    pick_v_ref[pl.ds(start, own), :] = picked

    return kernel_call(
        body,
        [shape((2 * rows, LANES)), shape((rows, LANES))],
        "route_lanes",
        1 << 24,
        scalars=1,
    )(info, *codes)


def project(ring, info, near, far, table, pick_v, pick_o, position_bias, window):
    _, own, width = near.shape
    own //= 2
    rows = own * 4
    key_count = rows * 2
    count = len(ring.blocks)
    head_width = position_bias.shape[1]

    def body(info_ref, *refs):
        block_refs, refs = refs[:count], refs[count:]
        near_ref, far_ref, table_ref, pick_v_ref, pick_o_ref, pos_ref = refs[:6]
        (w_ref, a_ref, key_ref, value_ref, gate_ref, expert_ref) = refs[6:12]
        (qu_ref, qv_ref, ogate_ref, rel_ref) = refs[12:]
        lay_columns(w_ref, block_refs, ring.pieces, info_ref, head_width)
        lane_index = lax.broadcasted_iota(jnp.int32, (own, LANES), 1)
        lane, last = lane_index < head_width, lane_index == LANES - 1
        slot = lax.broadcasted_iota(jnp.int32, (own, LANES), 0)
        place_bias = jnp.concatenate(
            [pos_ref[...], jnp.zeros((2, LANES - head_width), F32)], axis=1
        )
        for k in range(4):
            place = (info_ref[0] ^ k) * own
            for current in range(2):
                row = pl.multiple_of(place + current * rows, 16)
                there = pl.ds(row, own)
                a = (far_ref if k // 2 else near_ref)[k % 2, current * own : (current + 1) * own, :]
                a_ref[there, :] = a
                keyval = mm_nt(a, w_ref[LANES : LANES + KEYVAL, :])
                logits = keyval[:, :LANES]
                pick = pick_v_ref[there, :].astype(F32)
                if current:
                    valid = pick > 0.5
                else:
                    valid = slot + place >= rows - info_ref[2]
                masked = jnp.where(last & jnp.logical_not(valid), NEG, 0.0)
                key_ref[there, :] = jnp.where(lane, logits, masked).astype(BF)
                gate = jnp.where(last, 0.0, pick) / (1.0 + jnp.exp(-logits))
                gate_ref[there, :] = gate
                expert_ref[there, :] = keyval[:, LANES:].astype(BF)
                total = jnp.zeros((own, LANES), F32)
                for e in range(EXPERTS):
                    block = keyval[:, LANES * (e + 1) : LANES * (e + 2)]
                    total = total + gate[:, head_width + e : head_width + e + 1] * block
                value_ref[there, :] = total.astype(BF)
                if current:
                    here = pl.ds(pl.multiple_of(place, 16), own)
                    query = mm_nt(a, w_ref[0:LANES, :])
                    mark = jnp.where(last, 1.0, 0.0)
                    qu_ref[here, :] = jnp.where(lane, query + place_bias[0:1, :], mark).astype(BF)
                    qv_ref[here, :] = jnp.where(lane, query + place_bias[1:2, :], 0.0).astype(BF)
                    ogate_ref[here, :] = pick_o_ref[here, :].astype(F32) / (1.0 + jnp.exp(-query))
        rel = mm_nt(table_ref[...], w_ref[LANES + KEYVAL : FIRST, :])
        rel_ref[0:key_count, :] = rel.astype(BF)
        rel_ref[key_count:, :] = jnp.zeros((window - key_count, LANES), BF)

    return kernel_call(
        body,
        [
            shape((FIRST + SPREAD, width)),
            shape((key_count, width)),
            shape((key_count, LANES)),
            shape((key_count, LANES)),
            shape((key_count, LANES), F32),
            shape((key_count, SPREAD)),
            shape((rows, LANES)),
            shape((rows, LANES)),
            shape((rows, LANES), F32),
            shape((window, LANES)),
        ],
        "projections",
        2 * key_count * width * (KEYVAL + 2 * LANES),
        scalars=1,
        spare=14,
    )(info, *ring.blocks, near, far, table, pick_v, pick_o, position_bias)


def block_plan(rows, slots, first=0, stop=None):
    keys = rows + slots
    plan = []
    stop = stop or rows
    while first < stop:
        size = min(256, stop - first)
        columns = min(-(-(slots + first + size) // LANES) * LANES, keys)
        start = (rows - first - size) // LANES * LANES
        turn = rows - 1 - first - start
        length = -(-(columns + turn + 1) // LANES) * LANES
        plan.append((first, size, columns, start, length, turn))
        first += size
    return plan


def window_rows(plan):
    return max(item[3] + item[4] for item in plan)


def attention_forward(plan, slots, factor, qu, qv, keys, values, rel):
    rows = qu.shape[0]
    key_count = keys.shape[0]

    def body(qu_ref, qv_ref, key_ref, value_ref, rel_ref, probs_ref, out_ref):
        for first, size, columns, start, length, turn in plan:
            here = slice(first, first + size)
            content = mm_nt(qu_ref[here, :], key_ref[0:columns, :])
            window = mm_nt(qv_ref[here, :], rel_ref[start : start + length, :])
            turned = pltpu.roll(window, length - turn, 1, stride=1, stride_axis=0)
            scores = (content + turned[:, :columns]) * factor
            column = lax.broadcasted_iota(jnp.int32, (size, columns), 1)
            row = lax.broadcasted_iota(jnp.int32, (size, columns), 0)
            scores = jnp.where(column <= slots + first + row, scores, NEG)
            top = jnp.max(scores, axis=1, keepdims=True)
            weights = jnp.exp2(scores - top)
            total = jnp.sum(weights, axis=1, keepdims=True)
            probs = (weights * (1.0 / total)).astype(BF)
            probs_ref[here, 0:columns] = probs
            out_ref[here, :] = mm(probs, value_ref[0:columns, :])

    return kernel_call(
        body,
        [shape((rows, key_count)), shape((rows, LANES), F32)],
        "attention_forward",
        10 * rows * key_count * LANES,
    )(qu, qv, keys, values, rel)


def out_projection(which, me, own, weights, att, ogate, head_width, name):
    width = weights.shape[1]
    count = len(which)

    def body(me_ref, w_ref, att_ref, ogate_ref, mixed_ref, out_ref):
        for index, k in enumerate(which):
            there = pl.ds(pl.multiple_of((me_ref[0] ^ k) * own, 16), own)
            att_block, gate = att_ref[there, :], ogate_ref[there, :]
            for e in range(EXPERTS):
                block = gate[:, head_width + e : head_width + e + 1] * att_block
                mixed_ref[index * own : (index + 1) * own, LANES * e : LANES * (e + 1)] = (
                    block.astype(BF)
                )
        result = mm(mixed_ref[...], w_ref[FIRST:, :]).astype(BF)
        for index in range(count):
            out_ref[index] = result[index * own : (index + 1) * own, :]

    return kernel_call(
        body,
        [shape((count * own, SPREAD)), shape((count, own, width))],
        name,
        2 * count * own * width * SPREAD,
        scalars=1,
    )(me, weights, att, ogate)


def lane_sums(head_width):
    row = lax.broadcasted_iota(jnp.int32, (SPREAD, LANES), 0)
    column = lax.broadcasted_iota(jnp.int32, (SPREAD, LANES), 1)
    first = (column - head_width) * LANES
    return jnp.where((row >= first) & (row < first + LANES), 1.0, 0.0).astype(BF)


def attended_grads(which, me, parts, weights, att, ogate, head_width, name):
    own, width = parts[0].shape
    count = len(which)

    def body(me_ref, *refs):
        part_refs, refs = refs[:count], refs[count:]
        w_ref, att_ref, ogate_ref, datt_ref, dlogit_ref = refs
        sums = lane_sums(head_width)
        for index, k in enumerate(which):
            there = pl.ds(pl.multiple_of((me_ref[0] ^ k) * own, 16), own)
            d_mixed = mm_nt(part_refs[index][...], w_ref[FIRST:, :])
            att_block, gate = att_ref[there, :], ogate_ref[there, :]
            d_att = jnp.zeros((own, LANES), F32)
            products = []
            for e in range(EXPERTS):
                block = d_mixed[:, LANES * e : LANES * (e + 1)]
                d_att = d_att + gate[:, head_width + e : head_width + e + 1] * block
                products.append((att_block * block).astype(BF))
            d_gate = mm(jnp.concatenate(products, axis=1), sums)
            datt_ref[index] = d_att.astype(BF)
            dlogit_ref[index] = (d_gate * gate * (1.0 - gate)).astype(BF)

    return kernel_call(
        body,
        [shape((count, own, LANES)), shape((count, own, LANES))],
        name,
        2 * count * own * width * SPREAD,
        scalars=1,
    )(me, *parts, weights, att, ogate)


def value_grads(me, near, far, parts, mixed_own, mixed_pair, probs, vgate, expert, plan, head_width):
    _, own, _ = near[0].shape
    _, width = parts[0].shape
    rows, key_count = probs.shape

    def body(me_ref, *refs):
        part_refs, refs = refs[:4], refs[4:]
        near_refs, far_refs, refs = refs[0:2], refs[2:4], refs[4:]
        mixed_refs, refs = refs[:2], refs[2:]
        probs_ref, vgate_ref, expert_ref = refs[:3]
        branch_ref, datt_ref, dlogit_ref, dexpert_ref, dvlogit_ref, mixed_ref, value_acc = refs[3:]
        for k in range(4):
            there = pl.ds(pl.multiple_of((me_ref[0] ^ k) * own, 16), own)
            branch_ref[there, :] = part_refs[k][...]
            first = (k // 2) * own
            mixed_ref[there, :] = mixed_refs[k % 2][first : first + own, :]
            datt_ref[there, :] = (far_refs if k // 2 else near_refs)[0][k % 2]
            dlogit_ref[there, :] = (far_refs if k // 2 else near_refs)[1][k % 2]
        value_acc[...] = jnp.zeros_like(value_acc)
        for first, size, columns, _, _, _ in plan:
            here = slice(first, first + size)
            turned = datt_ref[here, :].astype(F32).T.astype(BF)
            value_acc[:, 0:columns] += mm(turned, probs_ref[here, 0:columns])
        sums = lane_sums(head_width)
        step_rows = 2 * LANES
        for first in range(0, key_count, step_rows):
            size = min(step_rows, key_count - first)
            here = slice(first, first + size)
            d_value = value_acc[:, here].T
            gate = vgate_ref[here, :]
            products = []
            for e in range(EXPERTS):
                columns = slice(LANES * e, LANES * (e + 1))
                d_expert = gate[:, head_width + e : head_width + e + 1] * d_value
                dexpert_ref[here, columns] = d_expert.astype(BF)
                products.append((expert_ref[here, columns].astype(F32) * d_value).astype(BF))
            d_gate = mm(jnp.concatenate(products, axis=1), sums)
            dvlogit_ref[here, :] = (d_gate * gate * (1.0 - gate)).astype(BF)

    return kernel_call(
        body,
        [
            shape((rows, width)),
            shape((rows, LANES)),
            shape((rows, LANES)),
            shape((key_count, SPREAD)),
            shape((key_count, LANES)),
            shape((rows, SPREAD)),
        ],
        "value_grads",
        6 * rows * key_count * LANES,
        scratch=[shape((LANES, key_count), F32)],
        scalars=1,
    )(me, *parts, *near, *far, mixed_own, mixed_pair, probs, vgate, expert)


def block_shapes(rows, columns, upper, lower):
    half = RING // 2
    whole = shape((rows, columns))
    far = [shape((count, columns)) for count in (upper, lower) if count]
    return [whole] * half + far + [whole] * (half - 1)


def block_list(outs):
    half = RING // 2
    far = list(outs[half : len(outs) - half + 1])
    return list(outs[:half]) + [None] + list(outs[len(outs) - half + 1 :]), far


def store_block(refs, offset, first, value, skip=0):
    half = RING // 2
    rows = value.shape[0]
    if offset != half:
        refs[offset if offset < half else offset + len(refs) - RING][first : first + rows, :] = value
        return
    start = -skip
    for ref in refs[half : len(refs) - half + 1]:
        stop = start + ref.shape[0]
        low, high = max(start, first), min(stop, first + rows)
        if low < high:
            ref[low - start : high - start, :] = value[low - first : high - first]
        start = stop


def column_grads(info, pairs, keep, part, upper, above, name):
    ring = lax.axis_size("dp") == RING
    width = pairs[0][1].shape[1]
    total = sum(rows for segments in keep for _, rows in segments)
    most = max(left.shape[1] for left, _ in pairs)
    longest = max(left.shape[0] for left, _ in pairs)
    flops = sum(2 * left.shape[0] * left.shape[1] * width for left, _ in pairs)
    skip = above.shape[0] if ring and above is not None else 0
    more = [above] if skip else []

    def body(info_ref, *refs):
        count = 2 * len(pairs)
        ins, outs, (turned, whole) = refs[:count], refs[count + len(more) : -2], refs[-2:]
        if skip:
            outs[RING // 2][0:skip, :] = refs[count][...]
        place = 0
        for index in range(len(pairs)):
            left_ref, right_ref = ins[2 * index], ins[2 * index + 1]
            depth, rows = left_ref.shape
            start = right_ref.shape[0] - depth
            for row in range(0, rows, LANES):
                block = left_ref[:, row : row + LANES].astype(F32)
                turned[row : row + LANES, 0:depth] = block.T.astype(BF)
            for column in range(0, width, 256):
                there = slice(column, column + 256)
                whole[0:rows, there] = mm(
                    turned[0:rows, 0:depth], right_ref[start:, there]
                ).astype(BF)
            for first, kept in keep[index]:
                if ring:
                    for offset in range(RING):
                        column = pl.multiple_of(ring_index(info_ref, offset) * part, LANES)
                        value = whole[first : first + kept, pl.ds(column, part)]
                        store_block(outs, offset, place, value, skip)
                else:
                    outs[0][place : place + kept, :] = whole[first : first + kept, :]
                place += kept

    shapes = [shape((total, width))]
    if ring:
        parts = (0, skip + total) if skip else (upper, total - upper)
        shapes = block_shapes(total, part, *parts)
    outs = kernel_call(
        body,
        shapes,
        name,
        flops,
        scratch=[shape((most, longest)), shape((most, width))],
        scalars=1,
    )(info, *[item for pair in pairs for item in pair], *more)
    return block_list(outs) if ring else (list(outs), [None, None])


def score_grads(first, stop_plan, refs, accs, scale, head_width):
    probs_ref, att_ref, qu_ref, qv_ref, key_ref, value_ref, rel_ref, grads_of, store = refs
    key_acc, rel_acc, sums_ref = accs
    for row_first, size, columns, start, length, turn in stop_plan:
        here = slice(row_first, row_first + size)
        row = lax.broadcasted_iota(jnp.int32, (size, size), 0)
        column = lax.broadcasted_iota(jnp.int32, (size, size), 1)
        mirror = jnp.where(row + column == size - 1, 1.0, 0.0).astype(BF)
        weights = probs_ref[here, 0:columns]
        grads = grads_of(row_first - first, size)
        dot_rows = jnp.sum(grads.astype(F32) * att_ref[here, :], axis=1, keepdims=True)
        d_probs = mm_nt(grads, value_ref[0:columns, :])
        d_scores = (weights.astype(F32) * (d_probs - dot_rows)).astype(BF)
        key_acc[:, 0:columns] += mm(qu_ref[here, :].astype(F32).T.astype(BF), d_scores)
        d_qu = mm(d_scores, key_ref[0:columns, :])
        mirrored = jnp.concatenate(
            [mm(mirror, d_scores), jnp.zeros((size, length - columns), F32)], axis=1
        )
        turned = pltpu.roll(mirrored, turn - size + 1, 1, stride=1, stride_axis=0).astype(BF)
        back = mm(turned, rel_ref[start : start + length, :])
        qv_mirrored = mm(mirror, qv_ref[here, :]).T.astype(BF)
        rel_acc[:, start : start + length] += mm(qv_mirrored, turned)
        high = back.astype(BF)
        low = (back - high.astype(F32)).astype(BF)
        d_qv = mm(mirror, high) + mm(mirror, low)
        store(row_first - first, size, ((d_qu + d_qv) * scale).astype(BF))
        sums_ref[0:1, :] += jnp.sum(d_qu, axis=0, keepdims=True) * scale
        sums_ref[1:2, :] += jnp.sum(d_qv, axis=0, keepdims=True) * scale


def score_grads_near(info, slots, scale, head_width, probs, d_att, d_ologit, att, qu, qv, keys, values, rel):
    rows = qu.shape[0]
    own = d_att.shape[1]
    key_count, window = keys.shape[0], rel.shape[0]
    half = 2 * own
    plans = [block_plan(rows, slots, x * half, (x + 1) * half) for x in range(2)]

    def body(info_ref, probs_ref, datt_ref, ologit_ref, att_ref, qu_ref, qv_ref, key_ref, value_ref, rel_ref, dq_ref, key_acc, rel_acc, sums_ref, grads_all, logits_all):
        key_acc[...] = jnp.zeros_like(key_acc)
        rel_acc[...] = jnp.zeros_like(rel_acc)
        sums_ref[...] = jnp.zeros_like(sums_ref)
        core = info_ref[0] & 1
        for k in range(2):
            grads_all[k * own : (k + 1) * own, :] = datt_ref[core ^ k]
            logits_all[k * own : (k + 1) * own, :] = ologit_ref[core ^ k]

        def grads_of(first, size):
            return grads_all[first : first + size, :]

        def store(first, size, value):
            lane = lax.broadcasted_iota(jnp.int32, (size, LANES), 1) < head_width
            there = slice(first, first + size)
            dq_ref[there, :] = jnp.where(lane, value, logits_all[there, :])

        for x in range(2):

            @pl.when(info_ref[0] >> 1 == x)
            def _(x=x):
                score_grads(
                    x * half,
                    plans[x],
                    (probs_ref, att_ref, qu_ref, qv_ref, key_ref, value_ref, rel_ref, grads_of, store),
                    (key_acc, rel_acc, sums_ref),
                    scale,
                    head_width,
                )

    return kernel_call(
        body,
        [
            shape((half, LANES)),
            shape((LANES, key_count), F32),
            shape((LANES, window), F32),
            shape((2, LANES), F32),
        ],
        "score_grads_near",
        7 * rows * key_count * LANES,
        scratch=[shape((half, LANES)), shape((half, LANES))],
        scalars=1,
    )(info, probs, d_att, d_ologit, att, qu, qv, keys, values, rel)


def score_grads_far(info, slots, scale, head_width, near, probs, d_att, d_ologit, d_vlogit, att, qu, qv, keys, values, rel):
    rows = qu.shape[0]
    key_count, window = keys.shape[0], rel.shape[0]
    half = rows // 2
    plans = [block_plan(rows, slots, x * half, (x + 1) * half) for x in range(2)]

    def body(info_ref, near_ref, near_key, near_rel, near_sums, probs_ref, datt_ref, ologit_ref, vlogit_ref, att_ref, qu_ref, qv_ref, key_ref, value_ref, rel_ref, dq_ref, dkey_ref, drel_ref, sums_ref, key_acc, rel_acc):
        key_acc[...] = near_key[...]
        rel_acc[...] = near_rel[...]
        sums_ref[...] = near_sums[...]
        for x in range(2):

            @pl.when(info_ref[0] >> 1 == x)
            def _(x=x):
                first = (1 - x) * half
                dq_ref[x * half : (x + 1) * half, :] = near_ref[...]

                def grads_of(start, size):
                    return datt_ref[first + start : first + start + size, :]

                def store(start, size, value):
                    lane = lax.broadcasted_iota(jnp.int32, (size, LANES), 1) < head_width
                    there = slice(first + start, first + start + size)
                    dq_ref[there, :] = jnp.where(lane, value, ologit_ref[there, :])

                score_grads(
                    first,
                    plans[1 - x],
                    (probs_ref, att_ref, qu_ref, qv_ref, key_ref, value_ref, rel_ref, grads_of, store),
                    (key_acc, rel_acc, sums_ref),
                    scale,
                    head_width,
                )

        lane = lax.broadcasted_iota(jnp.int32, (key_count, LANES), 1) < head_width
        dkey_ref[...] = jnp.where(lane, (key_acc[...].T * scale).astype(BF), vlogit_ref[...])
        drel_ref[...] = (rel_acc[:, 0:key_count].T * scale).astype(BF)

    return kernel_call(
        body,
        [
            shape((rows, LANES)),
            shape((key_count, LANES)),
            shape((key_count, LANES)),
            shape((2, LANES), F32),
        ],
        "score_grads_far",
        7 * rows * key_count * LANES,
        scratch=[shape((LANES, key_count), F32), shape((LANES, window), F32)],
        scalars=1,
    )(info, *near, probs, d_att, d_ologit, d_vlogit, att, qu, qv, keys, values, rel)


def input_grads(which, me, normed, weights, d_query, d_key, d_expert, name):
    width = normed.shape[1]
    count = len(which)
    current = d_query is not None
    rows = d_key.shape[0] // 2
    own = rows // 4

    def body(me_ref, *refs):
        a_ref, w_ref, dkey_ref, dexpert_ref, refs = refs[0], refs[1], refs[2], refs[3], refs[4:]
        gain = jnp.zeros((1, width), F32)
        bias = jnp.zeros((1, width), F32)
        for index, k in enumerate(which):
            place = (me_ref[0] ^ k) * own
            there = pl.ds(pl.multiple_of(place + (rows if current else 0), 16), own)
            grads = mm(dkey_ref[there, :], w_ref[LANES : 2 * LANES, :])
            grads = grads + mm(dexpert_ref[there, :], w_ref[2 * LANES : LANES + KEYVAL, :])
            if current:
                here = pl.ds(pl.multiple_of(place, 16), own)
                grads = grads + mm(refs[0][here, :], w_ref[0:LANES, :])
                refs[1][index] = grads.astype(BF)
            gain = gain + jnp.sum(grads * a_ref[there, :].astype(F32), axis=0, keepdims=True)
            bias = bias + jnp.sum(grads, axis=0, keepdims=True)
        refs[-1][0:1, :] = gain
        refs[-1][1:2, :] = bias

    outs = [shape((count, own, width))] if current else []
    return kernel_call(
        body,
        outs + [shape((2, width), F32)],
        name,
        2 * count * own * width * (KEYVAL + LANES),
        scalars=1,
    )(me, normed, weights, d_key, d_expert, *([d_query] if current else []))


def add_far(mine, mine_at, theirs, theirs_at):
    dims = mine.shape[-2:]

    def body(a_ref, b_ref, out_ref):
        a = a_ref[...] if mine_at is None else a_ref[mine_at]
        b = b_ref[...] if theirs_at is None else b_ref[theirs_at]
        out_ref[...] = (a.astype(F32) + b.astype(F32)).astype(BF)

    return kernel_call(body, [shape(dims)], "add_far", 4 * mine.size)(mine, theirs)[0]


def marked_squares(marks, value):
    square = value * value
    high = square.astype(BF)
    low = (square - high.astype(F32)).astype(BF)
    return mm(marks, high) + mm(marks, low)


def second_norm(hidden, near, pair, far, gain, bias, marks):
    own, width = hidden.shape

    def body(hidden_ref, near_ref, pair_ref, far_ref, gain_ref, bias_ref, marks_ref, mid_ref, a_ref, sums_ref):
        branch = near_ref[0].astype(F32) + pair_ref[0].astype(F32) + far_ref[...].astype(F32)
        middle = hidden_ref[...].astype(F32) + branch
        mid_ref[...] = middle
        a_ref[...] = norm_rows(middle, gain_ref[1:2, :], bias_ref[1:2, :])[2].astype(BF)
        row = marks_ref[...].astype(F32).astype(BF)
        sums_ref[0:1, :] = marked_squares(row, branch)
        sums_ref[1:2, :] = mm(row, jnp.ones((own, width), BF))

    return kernel_call(
        body,
        [shape((own, width), F32), shape((own, width)), shape((2, width), F32)],
        "second_norm",
        40 * own * width,
    )(hidden, near, pair, far, gain, bias, marks)


def gelu_parts(source):
    density = jnp.exp2(source * source * (-0.5 * math.log2(math.e)))
    t = 1.0 / (1.0 + (0.3275911 / math.sqrt(2.0)) * jnp.abs(source))
    series = (0.5 * 1.061405429) * t + (0.5 * -1.453152027)
    series = series * t + (0.5 * 1.421413741)
    series = series * t + (0.5 * -0.284496736)
    series = series * t + (0.5 * 0.254829592)
    tail = series * t * density
    phi = jnp.where(source >= 0.0, 1.0 - tail, tail)
    return phi, phi + source * density * (1.0 / math.sqrt(2.0 * math.pi))


def feed_forward(ring, weights, normed, grads, name):
    own, width = normed[0].shape
    sources = [weights] if ring is None else ring.blocks
    count = len(sources)
    part = sources[0].shape[0]
    hidden_units = part if ring is None or not ring.ring else RING * part
    rows = 2 * own
    chunk = 256

    def body(*refs):
        a_refs, g_refs, refs_out = refs[count : count + 2], refs[count + 2 : count + 4], refs[count + 4 :]
        d0, d1, inner_ref, dpre_ref = refs_out[:4]
        a_all, g_all = refs_out[-2:]
        w_ref = refs[0]
        if ring is not None:
            w_ref = refs_out[4]
            for ref, (offset, first) in zip(refs[:count], ring.pieces):
                start = offset * part + first
                w_ref[start : start + ref.shape[0], :] = ref[...]
        for k in range(2):
            a_all[k * own : (k + 1) * own, :] = a_refs[k][...]
            g_all[k * own : (k + 1) * own, :] = g_refs[k][...]
        for first in range(0, hidden_units, chunk):
            here = slice(first, first + chunk)
            pre = mm_nt(a_all[...], w_ref[here, 0:width])
            d_inner = mm_nt(g_all[...], w_ref[here, width:])
            phi, slope = gelu_parts(pre)
            inner_ref[:, here] = (pre * phi).astype(BF)
            dpre_ref[:, here] = (d_inner * slope).astype(BF)
        for column in range(0, width, chunk):
            there = slice(column, column + chunk)
            grads_in = mm(dpre_ref[...], w_ref[:, there]).astype(BF)
            d0[:, there], d1[:, there] = grads_in[:own], grads_in[own:]

    block = shape((own, width))
    outs = [block] * 2 + [shape((rows, hidden_units)), shape((rows, hidden_units))]
    if ring is not None:
        outs.append(shape((hidden_units, 2 * width)))
    return kernel_call(
        body,
        outs,
        name,
        6 * rows * width * hidden_units,
        scratch=[shape((rows, width)), shape((rows, width))],
    )(*sources, *normed, *grads)


def feed_forward_result(weights, inner, own):
    rows, hidden_units = inner[0].shape
    width = weights.shape[1] // 2
    chunk = 256

    def body(w_ref, *refs):
        ins, outs = refs[:2], refs[2:]
        for which in range(2):
            for column in range(0, width, chunk):
                there = slice(column, column + chunk)
                value = mm(ins[which][...], w_ref[:, width + column : width + column + chunk])
                for k in range(2):
                    outs[2 * which + k][:, there] = value[k * own : (k + 1) * own].astype(BF)

    return kernel_call(
        body,
        [shape((own, width))] * 4,
        "feed_forward_result",
        4 * rows * width * hidden_units,
    )(weights, *inner)


def feed_forward_grads(normed, grads, inner, d_pre):
    own, width = normed[0].shape
    rows, hidden_units = inner[0].shape
    chunk = 256
    ring = lax.axis_size("dp") == RING
    part = hidden_units // RING

    def body(*refs):
        sides = ((refs[10:12], refs[0:4], 0), (refs[8:10], refs[4:8], width))
        outs, (turned, right) = refs[12:-2], refs[-2:]
        for left_refs, right_refs, column in sides:
            for k in range(4):
                right[k * own : (k + 1) * own, :] = right_refs[k][...]
            for half in range(2):
                for first in range(0, hidden_units, LANES):
                    block = left_refs[half][:, first : first + LANES].astype(F32)
                    turned[first : first + LANES, half * rows : (half + 1) * rows] = (
                        block.T.astype(BF)
                    )
            for first in range(0, width, chunk):
                there = slice(column + first, column + first + chunk)
                value = mm(turned[...], right[:, first : first + chunk]).astype(BF)
                if not ring:
                    outs[0][:, there] = value
                    continue
                for offset in range(RING):
                    store_block(
                        [ref.at[:, there] for ref in outs],
                        offset,
                        0,
                        value[offset * part : (offset + 1) * part],
                    )

    outs = kernel_call(
        body,
        block_shapes(part, 2 * width, part // 2, part // 2)
        if ring
        else [shape((hidden_units, 2 * width))],
        "feed_forward_grads",
        8 * rows * width * hidden_units,
        scratch=[shape((hidden_units, 2 * rows)), shape((2 * rows, width))],
    )(*normed, *grads, *inner, *d_pre)
    return block_list(outs) if ring else (list(outs), [None, None])


def norm_back(unit, inverse, scaled):
    return inverse * (
        scaled
        - jnp.mean(scaled, axis=-1, keepdims=True)
        - unit * jnp.mean(scaled * unit, axis=-1, keepdims=True)
    )


def second_norm_back(middle, near, pair, far, out_grad, gain):
    own, width = middle.shape

    def body(mid_ref, near_ref, pair_ref, far_ref, grad_ref, gain_ref, dmid_ref, dbr_ref, sums_ref):
        grads = near_ref[...].astype(F32) + pair_ref[...].astype(F32) + far_ref[...].astype(F32)
        unit, inverse, _ = norm_rows(mid_ref[...], 1.0, 0.0)
        d_mid = grad_ref[...].astype(F32) + norm_back(unit, inverse, grads * gain_ref[1:2, :])
        dmid_ref[...] = d_mid
        dbr_ref[...] = d_mid.astype(BF)
        sums_ref[0:1, :] = jnp.sum(grads * unit, axis=0, keepdims=True)
        sums_ref[1:2, :] = jnp.sum(grads, axis=0, keepdims=True)

    return kernel_call(
        body,
        [shape((own, width), F32), shape((own, width)), shape((2, width), F32)],
        "second_norm_back",
        40 * own * width,
    )(middle, near, pair, far, out_grad, gain)


def first_norm_back(hidden, near, pair, far, d_mid, gain):
    own, width = hidden.shape

    def body(hidden_ref, near_ref, pair_ref, far_ref, dmid_ref, gain_ref, out_ref):
        grads = near_ref[1].astype(F32) + pair_ref[0].astype(F32) + far_ref[...].astype(F32)
        unit, inverse, _ = norm_rows(hidden_ref[...].astype(F32), 1.0, 0.0)
        out_ref[...] = dmid_ref[...] + norm_back(unit, inverse, grads * gain_ref[0:1, :])

    return kernel_call(body, [shape((own, width), F32)], "first_norm_back", 40 * own * width)(
        hidden, near, pair, far, d_mid, gain
    )[0]


def final_result(middle, near, pair, far, marks):
    own, width = middle.shape

    def body(mid_ref, near_ref, pair_ref, far_ref, marks_ref, out_ref, sums_ref):
        result = mid_ref[...] + (
            near_ref[...].astype(F32) + pair_ref[...].astype(F32) + far_ref[...].astype(F32)
        )
        out_ref[...] = result.astype(BF)
        sums_ref[...] = marked_squares(marks_ref[...].astype(F32).astype(BF), result)

    return kernel_call(
        body, [shape((own, width)), shape((1, width), F32)], "final_result", 10 * own * width
    )(middle, near, pair, far, marks)


def small_sums(info, sums_a, sums_b, sums_c, sums_two, bias_sums, branch_sums, result_sums, heads):
    width = sums_a.shape[1]
    lines = width // LANES

    def body(info_ref, a_ref, b_ref, c_ref, two_ref, pos_ref, branch_ref, result_ref, out_ref):
        first = a_ref[...] + b_ref[...] + c_ref[...]
        kinds = [
            first[0:1, :],
            first[1:2, :],
            two_ref[0:1, :],
            two_ref[1:2, :],
            branch_ref[0:1, :],
            branch_ref[1:2, :],
            result_ref[...],
        ]
        for index, kind in enumerate(kinds):
            for line in range(lines):
                row = index * lines + line
                out_ref[row : row + 1, :] = kind[:, line * LANES : (line + 1) * LANES]
        row = len(kinds) * lines
        for head in range(heads):
            out_ref[row + 2 * head : row + 2 * head + 2, :] = jnp.where(
                info_ref[0] == head, pos_ref[...], 0.0
            )

    return kernel_call(
        body, [shape((7 * lines + 2 * heads, LANES), F32)], "small_sums", 1 << 16, scalars=1
    )(info, sums_a, sums_b, sums_c, sums_two, bias_sums, branch_sums, result_sums)[0]


def small_outputs(info, smalls, gain, bias, heads, head_width):
    width = gain.shape[1]
    lines = width // LANES
    across = heads * head_width
    wide = -(-across // LANES) * LANES

    count = len(smalls)

    def body(info_ref, *refs):
        ins, refs = refs[:count], refs[count:]
        gain_ref, bias_ref, dgain_ref, dbias_ref, pos_ref, stats_ref, small_ref = refs
        if count == 1:
            small_ref[...] = ins[0][...]
        else:
            place = lax.rem(info_ref[1], RING)
            own = jnp.where(place < RING // 2, place, RING - 1 - place)
            total = jnp.zeros(small_ref.shape, F32)
            for index in range(count):
                item = ins[0][...]
                for k in range(1, count):
                    item = jnp.where(own ^ k == index, ins[k][...], item)
                total = total + item
            small_ref[...] = total

        def kind(index):
            return [
                small_ref[index * lines + line : index * lines + line + 1, :] for line in range(lines)
            ]

        products, first_bias, second_gain, second_bias, branch, tokens, result = map(kind, range(7))
        for line in range(lines):
            there = slice(line * LANES, (line + 1) * LANES)
            dgain_ref[0:1, there] = (
                products[line] - bias_ref[0:1, there] * first_bias[line]
            ) / gain_ref[0:1, there]
            dgain_ref[1:2, there] = second_gain[line]
            dbias_ref[0:1, there] = first_bias[line]
            dbias_ref[1:2, there] = second_bias[line]
        lane = lax.broadcasted_iota(jnp.int32, (2, LANES), 1)
        total = jnp.zeros((2, wide), F32)
        for head in range(heads):
            row = 7 * lines + 2 * head
            part = jnp.where(lane < head_width, small_ref[row : row + 2, :], 0.0)
            part = jnp.concatenate([part, jnp.zeros((2, wide - LANES), F32)], axis=1)
            total = total + (pltpu.roll(part, head * head_width, 1) if head else part)
        pos_ref[...] = total[:, 0:across]
        squares = []
        for rows in (result, branch):
            whole = rows[0]
            for row in rows[1:]:
                whole = whole + row
            squares.append(jnp.sum(whole, axis=1, keepdims=True))
        first = lax.broadcasted_iota(jnp.int32, (1, LANES), 1) == 0
        stats_ref[...] = jnp.sqrt(jnp.where(first, squares[0], squares[1]) / (width * tokens[0]))

    return kernel_call(
        body,
        [
            shape((2, width), F32),
            shape((2, width), F32),
            shape((2, across), F32),
            shape((1, LANES), F32),
        ],
        "small_outputs",
        1 << 16,
        scratch=[shape(smalls[0].shape, F32)],
        scalars=1,
    )(info, *smalls, gain, bias)


def sinusoid_reversed(length, model_width):
    frequency = np.exp(np.arange(0, model_width, 2) * (-math.log(10000.0) / model_width))
    angles = np.arange(length - 1, -1, -1)[:, None] * frequency[None, :]
    return jnp.asarray(np.concatenate([np.sin(angles), np.cos(angles)], axis=1).astype(BF))


def shards(
    hidden,
    memory,
    out_grad,
    valid_mask,
    memory_length,
    value_routes,
    out_routes,
    norm_gain,
    norm_bias,
    query_weight,
    key_weight,
    rel_weight,
    value_weight,
    value_router,
    out_router,
    out_weight,
    position_bias,
    up_weight,
    down_weight,
):
    me = lax.axis_index("head").astype(jnp.int32)
    info = jnp.stack([me, ring_place(), memory_length[0].astype(jnp.int32)])
    heads = lax.axis_size("head")
    _, own, width = hidden.shape
    head_width = query_weight.shape[1]
    rows = own * heads
    slots = memory.shape[1] * heads
    key_count = rows + slots
    part = query_weight.shape[0]
    scale = 1.0 / math.sqrt(head_width)
    plan = block_plan(rows, slots)
    window = window_rows(plan)
    hidden, memory, out_grad = hidden[0], memory[0], out_grad[0]

    packed, rows_own = pack_weights(
        info,
        query_weight.T,
        out_router.T,
        key_weight.T,
        value_router.T,
        value_weight.T,
        rel_weight.T,
        out_weight,
        memory,
        hidden,
    )
    ring_w = RingGather(packed, 1)
    ring_w.advance()
    rows_far, rows_pair = flip(rows_own, 2), flip(rows_own, 1)
    value_routes, out_routes, table = hold(
        value_routes, out_routes, sinusoid_reversed(key_count, width), packed
    )[:-1]
    codes = route_codes(
        value_routes[0].transpose(0, 2, 3, 1), out_routes[0].transpose(1, 2, 0), valid_mask
    )
    codes, rows_pair = ring_w.arrived(codes, rows_pair)
    ring_w.advance()
    codes_far = flip(codes, 2)
    codes_pair = flip(codes, 1)
    a_near = first_norm([rows_own, rows_pair], norm_gain, norm_bias, "first_norm_near")
    a_near, rows_far = ring_w.arrived(a_near, rows_far)
    ring_w.advance()
    rows_last = flip(rows_far, 1)
    a_far = first_norm([rows_far, rows_last], norm_gain, norm_bias, "first_norm_far")
    codes_last = flip(codes_far, 1)
    packed_ff = jnp.concatenate([up_weight, down_weight], axis=1)
    pick_v, pick_o = route_lanes(
        info, [codes, codes_pair, codes_far, codes_last], heads, head_width
    )
    a_far, packed_ff, pick_v, pick_o = ring_w.arrived(a_far, packed_ff, pick_v, pick_o)
    ring_w.advance()

    packed_ff, out_grad_sent = ring_w.arrived_last(packed_ff, out_grad)
    ring_f = RingGather(packed_ff, 0)
    ring_f.advance()
    grad_far = flip(out_grad_sent, 2)
    w_all, a_all, keys, values, vgate, expert, qu, qv, ogate, rel = project(
        ring_w, info, a_near, a_far, table, pick_v, pick_o, position_bias, window
    )
    qu, grad_far = ring_f.arrived(qu, grad_far)
    ring_f.advance()
    grad_parts = [out_grad, flip(out_grad_sent, 1), grad_far, flip(grad_far, 1)]
    probs, att = attention_forward(
        plan, slots, scale * math.log2(math.e), qu, qv, keys, values, rel
    )
    att, probs = ring_f.arrived(att, probs)
    ring_f.advance()
    mixed_pair, pair = out_projection(
        (1, 3), info, own, w_all, att, ogate, head_width, "out_projection_pair"
    )
    pair_in = flip(pair, 1)
    att, pair = hold(att, pair)
    mixed_own, near_far = out_projection(
        (0, 2), info, own, w_all, att, ogate, head_width, "out_projection_own"
    )
    pair_in, near_far = hold(pair_in, near_far)
    far_in = flip(add_far(near_far, 1, pair_in, 1), 2)
    (near_far,) = ring_f.arrived(near_far)
    ring_f.advance()
    middle, a_two, branch_sums = second_norm(
        hidden, near_far, pair_in, far_in, norm_gain, norm_bias, valid_mask
    )
    a_two_pair = flip(a_two, 1)
    a_two_far = flip(a_two, 2)
    (a_two_pair,) = ring_f.arrived_last(a_two_pair)

    d_near, d_pair, inner_near, dpre_near, w_ff = feed_forward(
        ring_f, None, [a_two, a_two_pair], grad_parts[:2], "feed_forward_near"
    )
    a_two_far, d_near, d_pair = hold(a_two_far, d_near, d_pair)
    d_pair = flip(d_pair, 1)
    a_parts = [a_two, a_two_pair, a_two_far, flip(a_two_far, 1)]
    d_far, d_last, inner_far, dpre_far = feed_forward(
        None, w_ff, a_parts[2:], grad_parts[2:], "feed_forward_far"
    )
    d_far_in = flip(add_far(d_far, None, flip(d_last, 1), None), 2)
    ff_blocks, ff_far = feed_forward_grads(
        a_parts, grad_parts, [inner_near, inner_far], [dpre_near, dpre_far]
    )
    y_near, y_pair, y_far, y_last = feed_forward_result(w_ff, [inner_near, inner_far], own)
    ring_g = RingSum([ff_blocks], *ff_far, 0)
    d_far_in, d_pair, y_near = ring_g.arrived(d_far_in, d_pair, y_near)
    d_mid, d_branch, sums_two = second_norm_back(
        middle, d_near, d_pair, d_far_in, out_grad, norm_gain
    )
    branch_far = flip(d_branch, 2)
    branch_pair = flip(d_branch, 1)
    ring_g.advance()

    branch_pair, y_pair, y_last = hold(branch_pair, y_pair, y_last)
    grads_near = attended_grads(
        (0, 1), info, [d_branch, branch_pair], w_all, att, ogate, head_width, "attended_grads_near"
    )
    y_pair = flip(y_pair, 1)
    y_last = flip(y_last, 1)
    scores_near = score_grads_near(
        info, slots, scale, head_width, probs, *grads_near, att, qu, qv, keys, values, rel
    )
    branch_far, near_a, near_b, y_last, near_query = ring_g.arrived(
        branch_far, *grads_near, y_last, scores_near[0]
    )
    ring_g.advance()
    branch_parts = [d_branch, branch_pair, branch_far, flip(branch_far, 1)]
    grads_far = attended_grads(
        (2, 3), info, branch_parts[2:], w_all, att, ogate, head_width, "attended_grads_far"
    )
    branch_all, d_att, d_ologit, d_expert, d_vlogit, mixed = value_grads(
        info,
        (near_a, near_b),
        grads_far,
        branch_parts,
        mixed_own,
        mixed_pair,
        probs,
        vgate,
        expert,
        plan,
        head_width,
    )
    experts = [(e * LANES, head_width) for e in range(EXPERTS)]
    kept = 2 * EXPERTS * head_width
    upper = tile_half(kept + 2 * LANES + head_width)
    value_blocks, (value_upper, value_lower) = column_grads(
        info,
        [(mixed, branch_all), (d_expert, a_all)],
        [experts, experts],
        part,
        upper,
        None,
        "out_and_value_grads",
    )
    d_att, value_blocks[0], y_far, y_last = ring_g.arrived(d_att, value_blocks[0], y_far, y_last)
    ring_g.advance()
    y_far_in = flip(add_far(y_far, None, y_last, None), 2)
    d_query, d_key, d_rel, bias_sums = score_grads_far(
        info,
        slots,
        scale,
        head_width,
        (near_query,) + tuple(scores_near[1:]),
        probs,
        d_att,
        d_ologit,
        d_vlogit,
        att,
        qu,
        qv,
        keys,
        values,
        rel,
    )
    d_query, d_key, d_rel, y_far_in = hold(d_query, d_key, d_rel, y_far_in)
    late_blocks, late_far = column_grads(
        info,
        [(d_query, a_all), (d_key, a_all), (d_rel, table)],
        [[(0, LANES)], [(0, LANES)], [(0, head_width)]],
        part,
        None,
        value_lower,
        "query_key_rel_grads",
    )
    d_query, d_key, late_far[0] = hold(d_query, d_key, late_far[0])
    ring_v = RingSum([value_blocks, late_blocks], value_upper, late_far[0], 1)
    sums_c = input_grads(
        (0, 1, 2, 3), info, a_all, w_all, None, d_key, d_expert, "memory_sums"
    )[0]
    out_hidden, result_sums = final_result(middle, y_near, y_pair, y_far_in, valid_mask)
    d_query, sums_c, result_sums = ring_g.arrived(
        *ring_v.arrived(d_query, sums_c, result_sums)
    )
    ring_v.advance()
    pair, sums_a = input_grads(
        (1, 3), info, a_all, w_all, d_query, d_key, d_expert, "input_grads_pair"
    )
    pair_in = flip(pair, 1)
    d_query, pair = hold(d_query, pair)
    far_near, sums_b = input_grads(
        (2, 0), info, a_all, w_all, d_query, d_key, d_expert, "input_grads_own"
    )
    far_in = add_far(far_near, 0, pair_in, 1)
    small = small_sums(
        info, sums_a, sums_b, sums_c, sums_two, bias_sums, branch_sums, result_sums, heads
    )
    small = small + flip(small, 1)
    small = small + flip(small, 2)
    small, far_in = hold(small, far_in)
    far_in = flip(far_in, 2)
    count = lax.axis_size("dp")
    if count == RING:
        small = sum_over_dp(small, 1)
        (small,) = ring_v.arrived(small)
        ring_v.advance()
        smalls = [small] + [
            lax.ppermute(small, "dp", [(i, i ^ bit) for i in range(count)]) for bit in (2, 4, 6)
        ]
        smalls = list(ring_v.arrived(*smalls))
        ring_v.advance()
    else:
        bit = 1
        while bit < count:
            small = sum_over_dp(small, bit)
            bit *= 2
        smalls = [small]
    in_grad = first_norm_back(hidden, far_near, pair_in, far_in, d_mid, norm_gain)
    up_grad, down_grad = ring_g.finish(
        [(0, 0, part, 0, width), (0, 0, part, width, width)], "up_and_down_sum"
    )
    gain_grad, bias_grad, position_grad, stats = small_outputs(
        info, smalls, norm_gain, norm_bias, heads, head_width
    )
    in_grad, gain_grad, up_grad = ring_v.arrived(in_grad, gain_grad, up_grad)
    end = LANES + head_width
    out_weight_grad, value_grad, *late = ring_v.finish(
        [
            (0, 0, kept // 2, 0, part),
            (0, kept // 2, kept // 2, 0, part),
            (1, 0, head_width, 0, part),
            (1, head_width, EXPERTS, 0, part),
            (1, LANES, head_width, 0, part),
            (1, end, EXPERTS, 0, part),
            (1, 2 * LANES, head_width, 0, part),
        ],
        "weight_sums",
    )
    return (
        out_hidden[None],
        in_grad[None],
        gain_grad,
        bias_grad,
        late[0].T,
        late[2].T,
        late[4].T,
        value_grad.T,
        late[3].T,
        late[1].T,
        out_weight_grad,
        position_grad,
        up_grad,
        down_grad,
        stats[0, :2],
    )


def solution(mesh):
    return jax.shard_map(
        shards,
        mesh=mesh,
        in_specs=(
            P("dp", "head", None),
            P("dp", "head", None),
            P("dp", "head", None),
            P("dp", "head"),
            P("dp"),
            P("dp", None, "head", None, None),
            P("dp", "head", None, None),
            P(),
            P(),
            P("dp", "head"),
            P("dp", "head"),
            P("dp", "head"),
            P("dp", "head"),
            P("dp", "head"),
            P("dp", "head"),
            P("head", "dp"),
            P(None, "head"),
            P(("dp", "head"), None),
            P(("dp", "head"), None),
        ),
        out_specs=(
            P("dp", "head", None),
            P("dp", "head", None),
            P(),
            P(),
            P("dp", "head"),
            P("dp", "head"),
            P("dp", "head"),
            P("dp", "head"),
            P("dp", "head"),
            P("dp", "head"),
            P("head", "dp"),
            P(),
            P(("dp", "head"), None),
            P(("dp", "head"), None),
            P(),
        ),
        check_vma=False,
    )
```

```python
import math

import jax
import jax.numpy as jnp
import numpy as np
from jax import lax
from jax.experimental import pallas as pl
from jax.experimental.pallas import tpu as pltpu
from jax.sharding import PartitionSpec as P

EXPERTS = 5
LANES = 128
NEG = -1e30
EPS = 1e-05
BF = jnp.bfloat16
F32 = jnp.float32
RING = 8
SPREAD = EXPERTS * LANES
KEYVAL = LANES + SPREAD
FIRST = 2 * LANES + SPREAD + LANES


def mm(left, right):
    return jnp.dot(left, right, preferred_element_type=F32)


def mm_tn(left, right):
    return lax.dot_general(left, right, (((0,), (0,)), ((), ())), preferred_element_type=F32)


def mm_nt(left, right):
    return lax.dot_general(left, right, (((1,), (1,)), ((), ())), preferred_element_type=F32)


def hold(*values):
    return lax.optimization_barrier(values)


def shape(dims, dtype=BF):
    return jax.ShapeDtypeStruct(tuple(dims), dtype)


def padded_bytes(item):
    dims = list(item.shape)
    size = jnp.dtype(item.dtype).itemsize
    dims[-1] = -(-dims[-1] // LANES) * LANES
    if len(dims) > 1:
        dims[-2] = -(-dims[-2] // 16) * 16
    return size * math.prod(dims)


def kernel_call(body, outs, name, flops, scratch=(), scalars=0, spare=7, hbm=(), copies=0):
    def call(*operands):
        smem = pl.BlockSpec(memory_space=pltpu.SMEM)
        vmem = pl.BlockSpec(memory_space=pltpu.VMEM)
        far = pl.BlockSpec(memory_space=pltpu.HBM)
        total = sum(padded_bytes(item) for item in scratch)
        spaces = [pltpu.VMEM(x.shape, x.dtype) for x in scratch]
        if copies:
            spaces.append(pltpu.SemaphoreType.DMA((copies,)))
        return pl.pallas_call(
            body,
            out_shape=tuple(outs),
            in_specs=[
                smem if i < scalars else far if i in hbm else vmem for i in range(len(operands))
            ],
            out_specs=tuple(vmem for _ in outs),
            scratch_shapes=spaces,
            compiler_params=pltpu.CompilerParams(vmem_limit_bytes=total + (spare << 20)),
            cost_estimate=pl.CostEstimate(
                flops=int(flops) // 16, bytes_accessed=1 << 10, transcendentals=0
            ),
            name=name,
        )(*operands)

    return call


def flip(value, bit):
    count = lax.axis_size("head")
    return lax.ppermute(value, "head", [(i, i ^ bit) for i in range(count)])


def ring_order(count):
    return list(range(0, count, 2)) + list(range(count - 1, 0, -2))


def ring_place():
    index = lax.axis_index("dp")
    count = lax.axis_size("dp")
    return jnp.where(index & 1 == 0, index >> 1, count - 1 - (index >> 1)).astype(jnp.int32)


def ring_index(info_ref, offset):
    place = lax.rem(info_ref[1] + offset, RING)
    return jnp.where(place < RING // 2, 2 * place, 2 * RING - 1 - 2 * place)


def step(value, direction):
    count = lax.axis_size("dp")
    order = ring_order(count)
    return lax.ppermute(
        value, "dp", [(order[i], order[(i + direction) % count]) for i in range(count)]
    )


def tile_half(rows):
    return -(-(rows // 2) // 16) * 16


class RingGather:
    def __init__(self, own, axis):
        self.ring = lax.axis_size("dp") == RING
        self.half = tile_half(own.shape[0])
        self.round = 0
        if self.ring:
            self.blocks = [own]
            self.pieces = [(0, 0)]
            self.right, self.left = own, own
        else:
            self.blocks = [lax.all_gather(own, "dp", axis=axis, tiled=True)]
            self.pieces = [(0, 0)]

    def advance(self):
        if not self.ring or self.round == RING // 2:
            return
        self.round += 1
        k, half = self.round, self.half
        if k < RING // 2:
            self.right, self.left = step(self.right, 1), step(self.left, -1)
            self.pieces += [(RING - k, 0), (k, 0)]
        else:
            self.right, self.left = step(self.right[:half], 1), step(self.left[half:], -1)
            self.pieces += [(k, 0), (k, half)]
        self.blocks += [self.right, self.left]

    def arrived(self, *values):
        if not self.ring:
            return values
        out = hold(*values, self.right, self.left)
        self.right, self.left = out[-2:]
        self.blocks[-2:] = [self.right, self.left]
        return out[:-2]

    def arrived_last(self, *values):
        if not self.ring:
            return values
        return hold(*values, *self.blocks[-2:])[:-2]


def ring_add(ahead, right, behind, left):
    count = len(ahead)
    heights = [block.shape[0] for block in ahead]
    total = sum(heights)
    width = ahead[0].shape[1]

    def lay(out_ref, refs, got_ref, start):
        stop = start + got_ref.shape[0]
        first = 0
        for ref, rows in zip(refs, heights):
            low, high = max(start, first), min(stop, first + rows)
            if low < high:
                value = ref[low - first : high - first, :].astype(F32)
                value = value + got_ref[low - start : high - start, :].astype(F32)
                out_ref[low:high, :] = value.astype(BF)
            for begin, end in ((first, min(start, first + rows)), (max(stop, first), first + rows)):
                if begin < end:
                    out_ref[begin:end, :] = ref[begin - first : end - first, :]
            first += rows

    def body(*refs):
        a_refs, r_ref = refs[:count], refs[count]
        b_refs, l_ref = refs[count + 1 : 2 * count + 1], refs[2 * count + 1]
        ahead_ref, behind_ref = refs[2 * count + 2 :]
        lay(ahead_ref, a_refs, r_ref, 0)
        lay(behind_ref, b_refs, l_ref, total - left.shape[0])

    return kernel_call(
        body, [shape((total, width))] * 2, "ring_add", 8 * total * width
    )(*ahead, right, *behind, left)


class RingSum:
    def __init__(self, groups, upper, lower, axis):
        self.groups = groups
        self.axis = axis
        self.ring = lax.axis_size("dp") == RING
        self.rest = 0
        if self.ring:
            self.rest = RING // 2 - 1
            self.right, self.left = step(upper, 1), step(lower, -1)

    def advance(self):
        if not self.rest:
            return
        k = self.rest
        ahead, behind = ring_add(
            [blocks[k] for blocks in self.groups],
            self.right,
            [blocks[RING - k] for blocks in self.groups],
            self.left,
        )
        self.right, self.left = step(ahead, 1), step(behind, -1)
        self.rest -= 1

    def arrived(self, *values):
        if not self.ring:
            return values
        out = hold(*values, self.right, self.left)
        self.right, self.left = out[-2:]
        return out[:-2]

    def finish(self, outs, name):
        count = len(self.groups)
        if self.ring:
            while self.rest:
                self.advance()
            parts = [blocks[0] for blocks in self.groups] + [self.right, self.left]
        else:
            parts = [
                lax.psum_scatter(blocks[0], "dp", scatter_dimension=self.axis, tiled=True)
                for blocks in self.groups
            ]
        starts = [0]
        for part in parts[: count - 1]:
            starts.append(starts[-1] + part.shape[0])

        def body(*refs):
            ins, results = refs[: len(parts)], refs[len(parts) :]
            for result, (which, row, rows, column, columns) in zip(results, outs):
                across = slice(column, column + columns)
                total = ins[which][row : row + rows, across].astype(F32)
                first = starts[which] + row
                for ref in ins[count:]:
                    total = total + ref[first : first + rows, across].astype(F32)
                result[...] = total

        shapes = [shape((cuts[2], cuts[4]), F32) for cuts in outs]
        return kernel_call(body, shapes, name, 8 * parts[0].size)(*parts)


def sum_over_dp(value, bit):
    count = lax.axis_size("dp")
    return value + lax.ppermute(value, "dp", [(i, i ^ bit) for i in range(count)])


def packed_rows(head_width):
    inside = EXPERTS * head_width
    items = [(0, 0, LANES), (LANES, LANES, LANES)]
    for e in range(EXPERTS):
        items.append((2 * LANES + e * head_width, (2 + e) * LANES, head_width))
    items.append((2 * LANES + inside, LANES + KEYVAL, head_width))
    for e in range(EXPERTS):
        items.append((2 * LANES + inside + (1 + e) * head_width, FIRST + e * LANES, head_width))
    return items


def lay_columns(whole, refs, pieces, info_ref, head_width):
    total = whole.shape[1]
    items = packed_rows(head_width)
    for _, target, rows in items:
        if rows < LANES:
            whole[target + rows : target + LANES, :] = jnp.zeros((LANES - rows, total), BF)
    for ref, (offset, start) in zip(refs, pieces):
        height, width = ref.shape
        for source, target, rows in items:
            low, high = max(source, start), min(source + rows, start + height)
            if low >= high:
                continue
            value = ref[low - start : high - start, :]
            there = slice(target + low - source, target + high - source)
            if width == total:
                whole[there, :] = value
            else:
                column = pl.multiple_of(ring_index(info_ref, offset) * width, LANES)
                whole[there, pl.ds(column, width)] = value


def norm_rows(source, gain, bias):
    center = source - jnp.mean(source, axis=-1, keepdims=True)
    inverse = lax.rsqrt(jnp.mean(center * center, axis=-1, keepdims=True) + EPS)
    unit = center * inverse
    return unit, inverse, unit * gain + bias


def pack_weights(info, query, out_router, key, value_router, value, rel, out_weight, memory, hidden):
    part = query.shape[1]
    head_width = query.shape[0]
    tail = LANES - head_width

    own, width = hidden.shape

    def body(
        info_ref, q_ref, or_ref, k_ref, vr_ref, v_ref, r_ref, o_ref, m_ref, h_ref, out_ref, rows_ref, routers, sems
    ):
        moves = [(or_ref, routers.at[0]), (vr_ref, routers.at[1])]
        first = 2 * LANES
        for ref in (v_ref, r_ref, o_ref):
            moves.append((ref, out_ref.at[first : first + ref.shape[0], :]))
            first += ref.shape[0]
        for ref, first in ((q_ref, 0), (k_ref, LANES)):
            moves.append((ref, out_ref.at[first : first + head_width, :]))
        moves += [(m_ref, rows_ref.at[0:own, :]), (h_ref, rows_ref.at[own : 2 * own, :])]
        started = []
        for index, (source, target) in enumerate(moves):
            copy = pltpu.make_async_copy(source, target, sems.at[index])
            copy.start()
            started.append(copy)
        started[0].wait()
        started[1].wait()
        for index in range(2):
            rest = jnp.concatenate(
                [routers[index].astype(F32), jnp.zeros((tail - EXPERTS, part), F32)], axis=0
            )
            first = LANES * index + head_width
            out_ref[first : first + tail, :] = rest.astype(BF)
        for copy in started[2:]:
            copy.wait()

    return kernel_call(
        body,
        [shape((2 * LANES + (2 * EXPERTS + 1) * head_width, part)), shape((2 * own, width))],
        "pack_weights",
        1 << 20,
        scratch=[shape((2, EXPERTS, part))],
        scalars=1,
        spare=54,
        hbm=tuple(range(1, 10)),
        copies=9,
    )(info, query, out_router, key, value_router, value, rel, out_weight, memory, hidden)


def first_norm(parts, gain, bias, name):
    rows, width = parts[0].shape
    count = len(parts)

    def body(*refs):
        gain_ref, bias_ref, out_ref = refs[count:]
        for k in range(count):
            source = refs[k][...].astype(F32)
            out_ref[k] = norm_rows(source, gain_ref[0:1, :], bias_ref[0:1, :])[2].astype(BF)

    return kernel_call(
        body, [shape((count, rows, width))], name, count * 400 * rows * width
    )(*parts, gain, bias)[0]


def route_codes(value_routes, out_routes, valid_mask):
    heads, _, own = out_routes.shape
    lines = 6 * heads + 1
    total = -(-lines // 16) * 16

    def body(v_ref, o_ref, m_ref, out_ref):
        parts = [v_ref[kind, head].astype(F32) for kind in range(2) for head in range(heads)]
        parts += [o_ref[head].astype(F32) for head in range(heads)]
        parts += [m_ref[...].astype(F32), jnp.zeros((total - lines, own), F32)]
        out_ref[...] = jnp.concatenate(parts, axis=0).astype(BF)

    return kernel_call(body, [shape((total, own))], "route_codes", 1 << 16)(
        value_routes, out_routes, valid_mask
    )[0]


def route_lanes(info, codes, heads, head_width):
    lines, own = codes[0].shape
    rows = own * heads

    def body(info_ref, c0, c1, c2, c3, pick_v_ref, pick_o_ref):
        row = lax.broadcasted_iota(jnp.int32, (own, own), 0)
        same = jnp.where(row == lax.broadcasted_iota(jnp.int32, (own, own), 1), 1.0, 0.0).astype(BF)
        expert = lax.broadcasted_iota(jnp.int32, (LANES, own), 0) - head_width
        expert = expert.astype(F32)
        last = lax.broadcasted_iota(jnp.int32, (LANES, own), 0) == LANES - 1
        for k, ref in enumerate((c0, c1, c2, c3)):
            lines_all = ref[...].astype(F32)
            place = (info_ref[0] ^ k) * own
            for kind in range(3):
                named = []
                for choice in range(2):
                    line = jnp.zeros((1, own), F32)
                    for head in range(heads):
                        at = (kind * heads + head) * 2 + choice
                        line = line + jnp.where(
                            info_ref[0] == head, lines_all[at : at + 1, :], 0.0
                        )
                    named.append(line)
                hit = (expert == named[0]) | (expert == named[1])
                lanes = jnp.where(hit, 1.0, 0.0)
                if kind == 1:
                    lanes = jnp.where(last, lines_all[6 * heads : 6 * heads + 1, :], lanes)
                picked = mm_nt(same, lanes.astype(BF)).astype(BF)
                if kind == 2:
                    pick_o_ref[pl.ds(pl.multiple_of(place, 16), own), :] = picked
                else:
                    start = pl.multiple_of(place + kind * rows, 16)
                    pick_v_ref[pl.ds(start, own), :] = picked

    return kernel_call(
        body,
        [shape((2 * rows, LANES)), shape((rows, LANES))],
        "route_lanes",
        1 << 24,
        scalars=1,
    )(info, *codes)


def project(ring, info, near, far, table, pick_v, pick_o, position_bias, window):
    _, own, width = near.shape
    own //= 2
    rows = own * 4
    key_count = rows * 2
    count = len(ring.blocks)
    head_width = position_bias.shape[1]

    def body(info_ref, *refs):
        block_refs, refs = refs[:count], refs[count:]
        near_ref, far_ref, table_ref, pick_v_ref, pick_o_ref, pos_ref = refs[:6]
        (w_ref, a_ref, key_ref, value_ref, gate_ref, expert_ref) = refs[6:12]
        (qu_ref, qv_ref, ogate_ref, rel_ref) = refs[12:]
        lay_columns(w_ref, block_refs, ring.pieces, info_ref, head_width)
        lane_index = lax.broadcasted_iota(jnp.int32, (own, LANES), 1)
        lane, last = lane_index < head_width, lane_index == LANES - 1
        slot = lax.broadcasted_iota(jnp.int32, (own, LANES), 0)
        place_bias = jnp.concatenate(
            [pos_ref[...], jnp.zeros((2, LANES - head_width), F32)], axis=1
        )
        for k in range(4):
            place = (info_ref[0] ^ k) * own
            for current in range(2):
                row = pl.multiple_of(place + current * rows, 16)
                there = pl.ds(row, own)
                a = (far_ref if k // 2 else near_ref)[k % 2, current * own : (current + 1) * own, :]
                a_ref[there, :] = a
                keyval = mm_nt(a, w_ref[LANES : LANES + KEYVAL, :])
                logits = keyval[:, :LANES]
                pick = pick_v_ref[there, :].astype(F32)
                if current:
                    valid = pick > 0.5
                else:
                    valid = slot + place >= rows - info_ref[2]
                masked = jnp.where(last & jnp.logical_not(valid), NEG, 0.0)
                key_ref[there, :] = jnp.where(lane, logits, masked).astype(BF)
                gate = jnp.where(last, 0.0, pick) / (1.0 + jnp.exp(-logits))
                gate_ref[there, :] = gate
                expert_ref[there, :] = keyval[:, LANES:].astype(BF)
                total = jnp.zeros((own, LANES), F32)
                for e in range(EXPERTS):
                    block = keyval[:, LANES * (e + 1) : LANES * (e + 2)]
                    total = total + gate[:, head_width + e : head_width + e + 1] * block
                value_ref[there, :] = total.astype(BF)
                if current:
                    here = pl.ds(pl.multiple_of(place, 16), own)
                    query = mm_nt(a, w_ref[0:LANES, :])
                    mark = jnp.where(last, 1.0, 0.0)
                    qu_ref[here, :] = jnp.where(lane, query + place_bias[0:1, :], mark).astype(BF)
                    qv_ref[here, :] = jnp.where(lane, query + place_bias[1:2, :], 0.0).astype(BF)
                    ogate_ref[here, :] = pick_o_ref[here, :].astype(F32) / (1.0 + jnp.exp(-query))
        rel = mm_nt(table_ref[...], w_ref[LANES + KEYVAL : FIRST, :])
        rel_ref[0:key_count, :] = rel.astype(BF)
        rel_ref[key_count:, :] = jnp.zeros((window - key_count, LANES), BF)

    return kernel_call(
        body,
        [
            shape((FIRST + SPREAD, width)),
            shape((key_count, width)),
            shape((key_count, LANES)),
            shape((key_count, LANES)),
            shape((key_count, LANES), F32),
            shape((key_count, SPREAD)),
            shape((rows, LANES)),
            shape((rows, LANES)),
            shape((rows, LANES), F32),
            shape((window, LANES)),
        ],
        "projections",
        2 * key_count * width * (KEYVAL + 2 * LANES),
        scalars=1,
        spare=14,
    )(info, *ring.blocks, near, far, table, pick_v, pick_o, position_bias)


def block_plan(rows, slots, first=0, stop=None):
    keys = rows + slots
    plan = []
    stop = stop or rows
    while first < stop:
        size = min(256, stop - first)
        columns = min(-(-(slots + first + size) // LANES) * LANES, keys)
        start = (rows - first - size) // LANES * LANES
        turn = rows - 1 - first - start
        length = -(-(columns + turn + 1) // LANES) * LANES
        plan.append((first, size, columns, start, length, turn))
        first += size
    return plan


def window_rows(plan):
    return max(item[3] + item[4] for item in plan)


def attention_forward(plan, slots, factor, qu, qv, keys, values, rel):
    rows = qu.shape[0]
    key_count = keys.shape[0]

    def body(qu_ref, qv_ref, key_ref, value_ref, rel_ref, probs_ref, out_ref):
        for first, size, columns, start, length, turn in plan:
            here = slice(first, first + size)
            content = mm_nt(qu_ref[here, :], key_ref[0:columns, :])
            window = mm_nt(qv_ref[here, :], rel_ref[start : start + length, :])
            turned = pltpu.roll(window, length - turn, 1, stride=1, stride_axis=0)
            scores = (content + turned[:, :columns]) * factor
            column = lax.broadcasted_iota(jnp.int32, (size, columns), 1)
            row = lax.broadcasted_iota(jnp.int32, (size, columns), 0)
            scores = jnp.where(column <= slots + first + row, scores, NEG)
            top = jnp.max(scores, axis=1, keepdims=True)
            weights = jnp.exp2(scores - top)
            total = jnp.sum(weights, axis=1, keepdims=True)
            probs = (weights * (1.0 / total)).astype(BF)
            probs_ref[here, 0:columns] = probs
            out_ref[here, :] = mm(probs, value_ref[0:columns, :])

    return kernel_call(
        body,
        [shape((rows, key_count)), shape((rows, LANES), F32)],
        "attention_forward",
        10 * rows * key_count * LANES,
    )(qu, qv, keys, values, rel)


def out_projection(which, me, own, weights, att, ogate, head_width, name):
    width = weights.shape[1]
    count = len(which)

    def body(me_ref, w_ref, att_ref, ogate_ref, mixed_ref, out_ref):
        for index, k in enumerate(which):
            there = pl.ds(pl.multiple_of((me_ref[0] ^ k) * own, 16), own)
            att_block, gate = att_ref[there, :], ogate_ref[there, :]
            for e in range(EXPERTS):
                block = gate[:, head_width + e : head_width + e + 1] * att_block
                mixed_ref[index * own : (index + 1) * own, LANES * e : LANES * (e + 1)] = (
                    block.astype(BF)
                )
        result = mm(mixed_ref[...], w_ref[FIRST:, :]).astype(BF)
        for index in range(count):
            out_ref[index] = result[index * own : (index + 1) * own, :]

    return kernel_call(
        body,
        [shape((count * own, SPREAD)), shape((count, own, width))],
        name,
        2 * count * own * width * SPREAD,
        scalars=1,
    )(me, weights, att, ogate)


def lane_sums(head_width):
    row = lax.broadcasted_iota(jnp.int32, (SPREAD, LANES), 0)
    column = lax.broadcasted_iota(jnp.int32, (SPREAD, LANES), 1)
    first = (column - head_width) * LANES
    return jnp.where((row >= first) & (row < first + LANES), 1.0, 0.0).astype(BF)


def attended_grads(which, me, parts, weights, att, ogate, head_width, name):
    own, width = parts[0].shape
    count = len(which)

    def body(me_ref, *refs):
        part_refs, refs = refs[:count], refs[count:]
        w_ref, att_ref, ogate_ref, datt_ref, dlogit_ref = refs
        sums = lane_sums(head_width)
        for index, k in enumerate(which):
            there = pl.ds(pl.multiple_of((me_ref[0] ^ k) * own, 16), own)
            d_mixed = mm_nt(part_refs[index][...], w_ref[FIRST:, :])
            att_block, gate = att_ref[there, :], ogate_ref[there, :]
            d_att = jnp.zeros((own, LANES), F32)
            products = []
            for e in range(EXPERTS):
                block = d_mixed[:, LANES * e : LANES * (e + 1)]
                d_att = d_att + gate[:, head_width + e : head_width + e + 1] * block
                products.append((att_block * block).astype(BF))
            d_gate = mm(jnp.concatenate(products, axis=1), sums)
            datt_ref[index] = d_att.astype(BF)
            dlogit_ref[index] = (d_gate * gate * (1.0 - gate)).astype(BF)

    return kernel_call(
        body,
        [shape((count, own, LANES)), shape((count, own, LANES))],
        name,
        2 * count * own * width * SPREAD,
        scalars=1,
    )(me, *parts, weights, att, ogate)


def value_grads(me, near, far, parts, mixed_own, mixed_pair, probs, vgate, expert, plan, head_width):
    _, own, _ = near[0].shape
    _, width = parts[0].shape
    rows, key_count = probs.shape

    def body(me_ref, *refs):
        part_refs, refs = refs[:4], refs[4:]
        near_refs, far_refs, refs = refs[0:2], refs[2:4], refs[4:]
        mixed_refs, refs = refs[:2], refs[2:]
        probs_ref, vgate_ref, expert_ref = refs[:3]
        branch_ref, datt_ref, dlogit_ref, dexpert_ref, dvlogit_ref, mixed_ref, value_acc = refs[3:]
        for k in range(4):
            there = pl.ds(pl.multiple_of((me_ref[0] ^ k) * own, 16), own)
            branch_ref[there, :] = part_refs[k][...]
            first = (k // 2) * own
            mixed_ref[there, :] = mixed_refs[k % 2][first : first + own, :]
            datt_ref[there, :] = (far_refs if k // 2 else near_refs)[0][k % 2]
            dlogit_ref[there, :] = (far_refs if k // 2 else near_refs)[1][k % 2]
        value_acc[...] = jnp.zeros_like(value_acc)
        for first, size, columns, _, _, _ in plan:
            here = slice(first, first + size)
            turned = datt_ref[here, :].astype(F32).T.astype(BF)
            value_acc[:, 0:columns] += mm(turned, probs_ref[here, 0:columns])
        sums = lane_sums(head_width)
        step_rows = 2 * LANES
        for first in range(0, key_count, step_rows):
            size = min(step_rows, key_count - first)
            here = slice(first, first + size)
            d_value = value_acc[:, here].T
            gate = vgate_ref[here, :]
            products = []
            for e in range(EXPERTS):
                columns = slice(LANES * e, LANES * (e + 1))
                d_expert = gate[:, head_width + e : head_width + e + 1] * d_value
                dexpert_ref[here, columns] = d_expert.astype(BF)
                products.append((expert_ref[here, columns].astype(F32) * d_value).astype(BF))
            d_gate = mm(jnp.concatenate(products, axis=1), sums)
            dvlogit_ref[here, :] = (d_gate * gate * (1.0 - gate)).astype(BF)

    return kernel_call(
        body,
        [
            shape((rows, width)),
            shape((rows, LANES)),
            shape((rows, LANES)),
            shape((key_count, SPREAD)),
            shape((key_count, LANES)),
            shape((rows, SPREAD)),
        ],
        "value_grads",
        6 * rows * key_count * LANES,
        scratch=[shape((LANES, key_count), F32)],
        scalars=1,
    )(me, *parts, *near, *far, mixed_own, mixed_pair, probs, vgate, expert)


def block_shapes(rows, columns, upper, lower):
    half = RING // 2
    whole = shape((rows, columns))
    far = [shape((count, columns)) for count in (upper, lower) if count]
    return [whole] * half + far + [whole] * (half - 1)


def block_list(outs):
    half = RING // 2
    far = list(outs[half : len(outs) - half + 1])
    return list(outs[:half]) + [None] + list(outs[len(outs) - half + 1 :]), far


def store_block(refs, offset, first, value, skip=0):
    half = RING // 2
    rows = value.shape[0]
    if offset != half:
        refs[offset if offset < half else offset + len(refs) - RING][first : first + rows, :] = value
        return
    start = -skip
    for ref in refs[half : len(refs) - half + 1]:
        stop = start + ref.shape[0]
        low, high = max(start, first), min(stop, first + rows)
        if low < high:
            ref[low - start : high - start, :] = value[low - first : high - first]
        start = stop


def column_grads(info, pairs, keep, part, upper, above, name):
    ring = lax.axis_size("dp") == RING
    width = pairs[0][1].shape[1]
    total = sum(rows for segments in keep for _, rows in segments)
    most = max(left.shape[1] for left, _ in pairs)
    longest = max(left.shape[0] for left, _ in pairs)
    flops = sum(2 * left.shape[0] * left.shape[1] * width for left, _ in pairs)
    skip = above.shape[0] if ring and above is not None else 0
    more = [above] if skip else []

    def body(info_ref, *refs):
        count = 2 * len(pairs)
        ins, outs, (turned, whole) = refs[:count], refs[count + len(more) : -2], refs[-2:]
        if skip:
            outs[RING // 2][0:skip, :] = refs[count][...]
        place = 0
        for index in range(len(pairs)):
            left_ref, right_ref = ins[2 * index], ins[2 * index + 1]
            depth, rows = left_ref.shape
            start = right_ref.shape[0] - depth
            for row in range(0, rows, LANES):
                block = left_ref[:, row : row + LANES].astype(F32)
                turned[row : row + LANES, 0:depth] = block.T.astype(BF)
            for column in range(0, width, 256):
                there = slice(column, column + 256)
                whole[0:rows, there] = mm(
                    turned[0:rows, 0:depth], right_ref[start:, there]
                ).astype(BF)
            for first, kept in keep[index]:
                if ring:
                    for offset in range(RING):
                        column = pl.multiple_of(ring_index(info_ref, offset) * part, LANES)
                        value = whole[first : first + kept, pl.ds(column, part)]
                        store_block(outs, offset, place, value, skip)
                else:
                    outs[0][place : place + kept, :] = whole[first : first + kept, :]
                place += kept

    shapes = [shape((total, width))]
    if ring:
        parts = (0, skip + total) if skip else (upper, total - upper)
        shapes = block_shapes(total, part, *parts)
    outs = kernel_call(
        body,
        shapes,
        name,
        flops,
        scratch=[shape((most, longest)), shape((most, width))],
        scalars=1,
    )(info, *[item for pair in pairs for item in pair], *more)
    return block_list(outs) if ring else (list(outs), [None, None])


def score_grads(first, stop_plan, refs, accs, scale, head_width):
    probs_ref, att_ref, qu_ref, qv_ref, key_ref, value_ref, rel_ref, grads_of, store = refs
    key_acc, rel_acc, sums_ref = accs
    for row_first, size, columns, start, length, turn in stop_plan:
        here = slice(row_first, row_first + size)
        row = lax.broadcasted_iota(jnp.int32, (size, size), 0)
        column = lax.broadcasted_iota(jnp.int32, (size, size), 1)
        mirror = jnp.where(row + column == size - 1, 1.0, 0.0).astype(BF)
        weights = probs_ref[here, 0:columns]
        grads = grads_of(row_first - first, size)
        dot_rows = jnp.sum(grads.astype(F32) * att_ref[here, :], axis=1, keepdims=True)
        d_probs = mm_nt(grads, value_ref[0:columns, :])
        d_scores = (weights.astype(F32) * (d_probs - dot_rows)).astype(BF)
        key_acc[:, 0:columns] += mm(qu_ref[here, :].astype(F32).T.astype(BF), d_scores)
        d_qu = mm(d_scores, key_ref[0:columns, :])
        mirrored = jnp.concatenate(
            [mm(mirror, d_scores), jnp.zeros((size, length - columns), F32)], axis=1
        )
        turned = pltpu.roll(mirrored, turn - size + 1, 1, stride=1, stride_axis=0).astype(BF)
        back = mm(turned, rel_ref[start : start + length, :])
        qv_mirrored = mm(mirror, qv_ref[here, :]).T.astype(BF)
        rel_acc[:, start : start + length] += mm(qv_mirrored, turned)
        high = back.astype(BF)
        low = (back - high.astype(F32)).astype(BF)
        d_qv = mm(mirror, high) + mm(mirror, low)
        store(row_first - first, size, ((d_qu + d_qv) * scale).astype(BF))
        sums_ref[0:1, :] += jnp.sum(d_qu, axis=0, keepdims=True) * scale
        sums_ref[1:2, :] += jnp.sum(d_qv, axis=0, keepdims=True) * scale


def score_grads_near(info, slots, scale, head_width, probs, d_att, d_ologit, att, qu, qv, keys, values, rel):
    rows = qu.shape[0]
    own = d_att.shape[1]
    key_count, window = keys.shape[0], rel.shape[0]
    half = 2 * own
    plans = [block_plan(rows, slots, x * half, (x + 1) * half) for x in range(2)]

    def body(info_ref, probs_ref, datt_ref, ologit_ref, att_ref, qu_ref, qv_ref, key_ref, value_ref, rel_ref, dq_ref, key_acc, rel_acc, sums_ref, grads_all, logits_all):
        key_acc[...] = jnp.zeros_like(key_acc)
        rel_acc[...] = jnp.zeros_like(rel_acc)
        sums_ref[...] = jnp.zeros_like(sums_ref)
        core = info_ref[0] & 1
        for k in range(2):
            grads_all[k * own : (k + 1) * own, :] = datt_ref[core ^ k]
            logits_all[k * own : (k + 1) * own, :] = ologit_ref[core ^ k]

        def grads_of(first, size):
            return grads_all[first : first + size, :]

        def store(first, size, value):
            lane = lax.broadcasted_iota(jnp.int32, (size, LANES), 1) < head_width
            there = slice(first, first + size)
            dq_ref[there, :] = jnp.where(lane, value, logits_all[there, :])

        for x in range(2):

            @pl.when(info_ref[0] >> 1 == x)
            def _(x=x):
                score_grads(
                    x * half,
                    plans[x],
                    (probs_ref, att_ref, qu_ref, qv_ref, key_ref, value_ref, rel_ref, grads_of, store),
                    (key_acc, rel_acc, sums_ref),
                    scale,
                    head_width,
                )

    return kernel_call(
        body,
        [
            shape((half, LANES)),
            shape((LANES, key_count), F32),
            shape((LANES, window), F32),
            shape((2, LANES), F32),
        ],
        "score_grads_near",
        7 * rows * key_count * LANES,
        scratch=[shape((half, LANES)), shape((half, LANES))],
        scalars=1,
    )(info, probs, d_att, d_ologit, att, qu, qv, keys, values, rel)


def score_grads_far(info, slots, scale, head_width, near, probs, d_att, d_ologit, d_vlogit, att, qu, qv, keys, values, rel):
    rows = qu.shape[0]
    key_count, window = keys.shape[0], rel.shape[0]
    half = rows // 2
    plans = [block_plan(rows, slots, x * half, (x + 1) * half) for x in range(2)]

    def body(info_ref, near_ref, near_key, near_rel, near_sums, probs_ref, datt_ref, ologit_ref, vlogit_ref, att_ref, qu_ref, qv_ref, key_ref, value_ref, rel_ref, dq_ref, dkey_ref, drel_ref, sums_ref, key_acc, rel_acc):
        key_acc[...] = near_key[...]
        rel_acc[...] = near_rel[...]
        sums_ref[...] = near_sums[...]
        for x in range(2):

            @pl.when(info_ref[0] >> 1 == x)
            def _(x=x):
                first = (1 - x) * half
                dq_ref[x * half : (x + 1) * half, :] = near_ref[...]

                def grads_of(start, size):
                    return datt_ref[first + start : first + start + size, :]

                def store(start, size, value):
                    lane = lax.broadcasted_iota(jnp.int32, (size, LANES), 1) < head_width
                    there = slice(first + start, first + start + size)
                    dq_ref[there, :] = jnp.where(lane, value, ologit_ref[there, :])

                score_grads(
                    first,
                    plans[1 - x],
                    (probs_ref, att_ref, qu_ref, qv_ref, key_ref, value_ref, rel_ref, grads_of, store),
                    (key_acc, rel_acc, sums_ref),
                    scale,
                    head_width,
                )

        lane = lax.broadcasted_iota(jnp.int32, (key_count, LANES), 1) < head_width
        dkey_ref[...] = jnp.where(lane, (key_acc[...].T * scale).astype(BF), vlogit_ref[...])
        drel_ref[...] = (rel_acc[:, 0:key_count].T * scale).astype(BF)

    return kernel_call(
        body,
        [
            shape((rows, LANES)),
            shape((key_count, LANES)),
            shape((key_count, LANES)),
            shape((2, LANES), F32),
        ],
        "score_grads_far",
        7 * rows * key_count * LANES,
        scratch=[shape((LANES, key_count), F32), shape((LANES, window), F32)],
        scalars=1,
    )(info, *near, probs, d_att, d_ologit, d_vlogit, att, qu, qv, keys, values, rel)


def input_grads(which, me, normed, weights, d_query, d_key, d_expert, name):
    width = normed.shape[1]
    count = len(which)
    current = d_query is not None
    rows = d_key.shape[0] // 2
    own = rows // 4

    def body(me_ref, *refs):
        a_ref, w_ref, dkey_ref, dexpert_ref, refs = refs[0], refs[1], refs[2], refs[3], refs[4:]
        gain = jnp.zeros((1, width), F32)
        bias = jnp.zeros((1, width), F32)
        for index, k in enumerate(which):
            place = (me_ref[0] ^ k) * own
            there = pl.ds(pl.multiple_of(place + (rows if current else 0), 16), own)
            grads = mm(dkey_ref[there, :], w_ref[LANES : 2 * LANES, :])
            grads = grads + mm(dexpert_ref[there, :], w_ref[2 * LANES : LANES + KEYVAL, :])
            if current:
                here = pl.ds(pl.multiple_of(place, 16), own)
                grads = grads + mm(refs[0][here, :], w_ref[0:LANES, :])
                refs[1][index] = grads.astype(BF)
            gain = gain + jnp.sum(grads * a_ref[there, :].astype(F32), axis=0, keepdims=True)
            bias = bias + jnp.sum(grads, axis=0, keepdims=True)
        refs[-1][0:1, :] = gain
        refs[-1][1:2, :] = bias

    outs = [shape((count, own, width))] if current else []
    return kernel_call(
        body,
        outs + [shape((2, width), F32)],
        name,
        2 * count * own * width * (KEYVAL + LANES),
        scalars=1,
    )(me, normed, weights, d_key, d_expert, *([d_query] if current else []))


def add_far(mine, mine_at, theirs, theirs_at):
    dims = mine.shape[-2:]

    def body(a_ref, b_ref, out_ref):
        a = a_ref[...] if mine_at is None else a_ref[mine_at]
        b = b_ref[...] if theirs_at is None else b_ref[theirs_at]
        out_ref[...] = (a.astype(F32) + b.astype(F32)).astype(BF)

    return kernel_call(body, [shape(dims)], "add_far", 4 * mine.size)(mine, theirs)[0]


def marked_squares(marks, value):
    square = value * value
    high = square.astype(BF)
    low = (square - high.astype(F32)).astype(BF)
    return mm(marks, high) + mm(marks, low)


def second_norm(hidden, near, pair, far, gain, bias, marks):
    own, width = hidden.shape

    def body(hidden_ref, near_ref, pair_ref, far_ref, gain_ref, bias_ref, marks_ref, mid_ref, a_ref, sums_ref):
        branch = near_ref[0].astype(F32) + pair_ref[0].astype(F32) + far_ref[...].astype(F32)
        middle = hidden_ref[...].astype(F32) + branch
        mid_ref[...] = middle
        a_ref[...] = norm_rows(middle, gain_ref[1:2, :], bias_ref[1:2, :])[2].astype(BF)
        row = marks_ref[...].astype(F32).astype(BF)
        sums_ref[0:1, :] = marked_squares(row, branch)
        sums_ref[1:2, :] = mm(row, jnp.ones((own, width), BF))

    return kernel_call(
        body,
        [shape((own, width), F32), shape((own, width)), shape((2, width), F32)],
        "second_norm",
        40 * own * width,
    )(hidden, near, pair, far, gain, bias, marks)


def gelu_parts(source):
    density = jnp.exp2(source * source * (-0.5 * math.log2(math.e)))
    t = 1.0 / (1.0 + (0.3275911 / math.sqrt(2.0)) * jnp.abs(source))
    series = (0.5 * 1.061405429) * t + (0.5 * -1.453152027)
    series = series * t + (0.5 * 1.421413741)
    series = series * t + (0.5 * -0.284496736)
    series = series * t + (0.5 * 0.254829592)
    tail = series * t * density
    phi = jnp.where(source >= 0.0, 1.0 - tail, tail)
    return phi, phi + source * density * (1.0 / math.sqrt(2.0 * math.pi))


def feed_forward(ring, weights, normed, grads, name):
    own, width = normed[0].shape
    sources = [weights] if ring is None else ring.blocks
    count = len(sources)
    part = sources[0].shape[0]
    hidden_units = part if ring is None or not ring.ring else RING * part
    rows = 2 * own
    chunk = 256

    def body(*refs):
        a_refs, g_refs, refs_out = refs[count : count + 2], refs[count + 2 : count + 4], refs[count + 4 :]
        d0, d1, inner_ref, dpre_ref = refs_out[:4]
        a_all, g_all = refs_out[-2:]
        w_ref = refs[0]
        if ring is not None:
            w_ref = refs_out[4]
            for ref, (offset, first) in zip(refs[:count], ring.pieces):
                start = offset * part + first
                w_ref[start : start + ref.shape[0], :] = ref[...]
        for k in range(2):
            a_all[k * own : (k + 1) * own, :] = a_refs[k][...]
            g_all[k * own : (k + 1) * own, :] = g_refs[k][...]
        for first in range(0, hidden_units, chunk):
            here = slice(first, first + chunk)
            pre = mm_nt(a_all[...], w_ref[here, 0:width])
            d_inner = mm_nt(g_all[...], w_ref[here, width:])
            phi, slope = gelu_parts(pre)
            inner_ref[:, here] = (pre * phi).astype(BF)
            dpre_ref[:, here] = (d_inner * slope).astype(BF)
        for column in range(0, width, chunk):
            there = slice(column, column + chunk)
            grads_in = mm(dpre_ref[...], w_ref[:, there]).astype(BF)
            d0[:, there], d1[:, there] = grads_in[:own], grads_in[own:]

    block = shape((own, width))
    outs = [block] * 2 + [shape((rows, hidden_units)), shape((rows, hidden_units))]
    if ring is not None:
        outs.append(shape((hidden_units, 2 * width)))
    return kernel_call(
        body,
        outs,
        name,
        6 * rows * width * hidden_units,
        scratch=[shape((rows, width)), shape((rows, width))],
    )(*sources, *normed, *grads)


def feed_forward_result(weights, inner, own):
    rows, hidden_units = inner[0].shape
    width = weights.shape[1] // 2
    chunk = 256

    def body(w_ref, *refs):
        ins, outs = refs[:2], refs[2:]
        for which in range(2):
            for column in range(0, width, chunk):
                there = slice(column, column + chunk)
                value = mm(ins[which][...], w_ref[:, width + column : width + column + chunk])
                for k in range(2):
                    outs[2 * which + k][:, there] = value[k * own : (k + 1) * own].astype(BF)

    return kernel_call(
        body,
        [shape((own, width))] * 4,
        "feed_forward_result",
        4 * rows * width * hidden_units,
    )(weights, *inner)


def feed_forward_grads(normed, grads, inner, d_pre):
    own, width = normed[0].shape
    rows, hidden_units = inner[0].shape
    chunk = 256
    ring = lax.axis_size("dp") == RING
    part = hidden_units // RING

    def body(*refs):
        sides = ((refs[10:12], refs[0:4], 0), (refs[8:10], refs[4:8], width))
        outs, (turned, right) = refs[12:-2], refs[-2:]
        for left_refs, right_refs, column in sides:
            for k in range(4):
                right[k * own : (k + 1) * own, :] = right_refs[k][...]
            for half in range(2):
                for first in range(0, hidden_units, LANES):
                    block = left_refs[half][:, first : first + LANES].astype(F32)
                    turned[first : first + LANES, half * rows : (half + 1) * rows] = (
                        block.T.astype(BF)
                    )
            for first in range(0, width, chunk):
                there = slice(column + first, column + first + chunk)
                value = mm(turned[...], right[:, first : first + chunk]).astype(BF)
                if not ring:
                    outs[0][:, there] = value
                    continue
                for offset in range(RING):
                    store_block(
                        [ref.at[:, there] for ref in outs],
                        offset,
                        0,
                        value[offset * part : (offset + 1) * part],
                    )

    outs = kernel_call(
        body,
        block_shapes(part, 2 * width, part // 2, part // 2)
        if ring
        else [shape((hidden_units, 2 * width))],
        "feed_forward_grads",
        8 * rows * width * hidden_units,
        scratch=[shape((hidden_units, 2 * rows)), shape((2 * rows, width))],
    )(*normed, *grads, *inner, *d_pre)
    return block_list(outs) if ring else (list(outs), [None, None])


def norm_back(unit, inverse, scaled):
    return inverse * (
        scaled
        - jnp.mean(scaled, axis=-1, keepdims=True)
        - unit * jnp.mean(scaled * unit, axis=-1, keepdims=True)
    )


def second_norm_back(middle, near, pair, far, out_grad, gain):
    own, width = middle.shape

    def body(mid_ref, near_ref, pair_ref, far_ref, grad_ref, gain_ref, dmid_ref, dbr_ref, sums_ref):
        grads = near_ref[...].astype(F32) + pair_ref[...].astype(F32) + far_ref[...].astype(F32)
        unit, inverse, _ = norm_rows(mid_ref[...], 1.0, 0.0)
        d_mid = grad_ref[...].astype(F32) + norm_back(unit, inverse, grads * gain_ref[1:2, :])
        dmid_ref[...] = d_mid
        dbr_ref[...] = d_mid.astype(BF)
        sums_ref[0:1, :] = jnp.sum(grads * unit, axis=0, keepdims=True)
        sums_ref[1:2, :] = jnp.sum(grads, axis=0, keepdims=True)

    return kernel_call(
        body,
        [shape((own, width), F32), shape((own, width)), shape((2, width), F32)],
        "second_norm_back",
        40 * own * width,
    )(middle, near, pair, far, out_grad, gain)


def first_norm_back(hidden, near, pair, far, d_mid, gain):
    own, width = hidden.shape

    def body(hidden_ref, near_ref, pair_ref, far_ref, dmid_ref, gain_ref, out_ref):
        grads = near_ref[1].astype(F32) + pair_ref[0].astype(F32) + far_ref[...].astype(F32)
        unit, inverse, _ = norm_rows(hidden_ref[...].astype(F32), 1.0, 0.0)
        out_ref[...] = dmid_ref[...] + norm_back(unit, inverse, grads * gain_ref[0:1, :])

    return kernel_call(body, [shape((own, width), F32)], "first_norm_back", 40 * own * width)(
        hidden, near, pair, far, d_mid, gain
    )[0]


def final_result(middle, near, pair, far, marks):
    own, width = middle.shape

    def body(mid_ref, near_ref, pair_ref, far_ref, marks_ref, out_ref, sums_ref):
        result = mid_ref[...] + (
            near_ref[...].astype(F32) + pair_ref[...].astype(F32) + far_ref[...].astype(F32)
        )
        out_ref[...] = result.astype(BF)
        sums_ref[...] = marked_squares(marks_ref[...].astype(F32).astype(BF), result)

    return kernel_call(
        body, [shape((own, width)), shape((1, width), F32)], "final_result", 10 * own * width
    )(middle, near, pair, far, marks)


def small_sums(info, sums_a, sums_b, sums_c, sums_two, bias_sums, branch_sums, result_sums, heads):
    width = sums_a.shape[1]
    lines = width // LANES

    def body(info_ref, a_ref, b_ref, c_ref, two_ref, pos_ref, branch_ref, result_ref, out_ref):
        first = a_ref[...] + b_ref[...] + c_ref[...]
        kinds = [
            first[0:1, :],
            first[1:2, :],
            two_ref[0:1, :],
            two_ref[1:2, :],
            branch_ref[0:1, :],
            branch_ref[1:2, :],
            result_ref[...],
        ]
        for index, kind in enumerate(kinds):
            for line in range(lines):
                row = index * lines + line
                out_ref[row : row + 1, :] = kind[:, line * LANES : (line + 1) * LANES]
        row = len(kinds) * lines
        for head in range(heads):
            out_ref[row + 2 * head : row + 2 * head + 2, :] = jnp.where(
                info_ref[0] == head, pos_ref[...], 0.0
            )

    return kernel_call(
        body, [shape((7 * lines + 2 * heads, LANES), F32)], "small_sums", 1 << 16, scalars=1
    )(info, sums_a, sums_b, sums_c, sums_two, bias_sums, branch_sums, result_sums)[0]


def small_outputs(info, smalls, gain, bias, heads, head_width):
    width = gain.shape[1]
    lines = width // LANES
    across = heads * head_width
    wide = -(-across // LANES) * LANES

    count = len(smalls)

    def body(info_ref, *refs):
        ins, refs = refs[:count], refs[count:]
        gain_ref, bias_ref, dgain_ref, dbias_ref, pos_ref, stats_ref, small_ref = refs
        if count == 1:
            small_ref[...] = ins[0][...]
        else:
            place = lax.rem(info_ref[1], RING)
            own = jnp.where(place < RING // 2, place, RING - 1 - place)
            total = jnp.zeros(small_ref.shape, F32)
            for index in range(count):
                item = ins[0][...]
                for k in range(1, count):
                    item = jnp.where(own ^ k == index, ins[k][...], item)
                total = total + item
            small_ref[...] = total

        def kind(index):
            return [
                small_ref[index * lines + line : index * lines + line + 1, :] for line in range(lines)
            ]

        products, first_bias, second_gain, second_bias, branch, tokens, result = map(kind, range(7))
        for line in range(lines):
            there = slice(line * LANES, (line + 1) * LANES)
            dgain_ref[0:1, there] = (
                products[line] - bias_ref[0:1, there] * first_bias[line]
            ) / gain_ref[0:1, there]
            dgain_ref[1:2, there] = second_gain[line]
            dbias_ref[0:1, there] = first_bias[line]
            dbias_ref[1:2, there] = second_bias[line]
        lane = lax.broadcasted_iota(jnp.int32, (2, LANES), 1)
        total = jnp.zeros((2, wide), F32)
        for head in range(heads):
            row = 7 * lines + 2 * head
            part = jnp.where(lane < head_width, small_ref[row : row + 2, :], 0.0)
            part = jnp.concatenate([part, jnp.zeros((2, wide - LANES), F32)], axis=1)
            total = total + (pltpu.roll(part, head * head_width, 1) if head else part)
        pos_ref[...] = total[:, 0:across]
        squares = []
        for rows in (result, branch):
            whole = rows[0]
            for row in rows[1:]:
                whole = whole + row
            squares.append(jnp.sum(whole, axis=1, keepdims=True))
        first = lax.broadcasted_iota(jnp.int32, (1, LANES), 1) == 0
        stats_ref[...] = jnp.sqrt(jnp.where(first, squares[0], squares[1]) / (width * tokens[0]))

    return kernel_call(
        body,
        [
            shape((2, width), F32),
            shape((2, width), F32),
            shape((2, across), F32),
            shape((1, LANES), F32),
        ],
        "small_outputs",
        1 << 16,
        scratch=[shape(smalls[0].shape, F32)],
        scalars=1,
    )(info, *smalls, gain, bias)


def sinusoid_reversed(length, model_width):
    frequency = np.exp(np.arange(0, model_width, 2) * (-math.log(10000.0) / model_width))
    angles = np.arange(length - 1, -1, -1)[:, None] * frequency[None, :]
    return jnp.asarray(np.concatenate([np.sin(angles), np.cos(angles)], axis=1).astype(BF))


def shards(
    hidden,
    memory,
    out_grad,
    valid_mask,
    memory_length,
    value_routes,
    out_routes,
    norm_gain,
    norm_bias,
    query_weight,
    key_weight,
    rel_weight,
    value_weight,
    value_router,
    out_router,
    out_weight,
    position_bias,
    up_weight,
    down_weight,
):
    me = lax.axis_index("head").astype(jnp.int32)
    info = jnp.stack([me, ring_place(), memory_length[0].astype(jnp.int32)])
    heads = lax.axis_size("head")
    _, own, width = hidden.shape
    head_width = query_weight.shape[1]
    rows = own * heads
    slots = memory.shape[1] * heads
    key_count = rows + slots
    part = query_weight.shape[0]
    scale = 1.0 / math.sqrt(head_width)
    plan = block_plan(rows, slots)
    window = window_rows(plan)
    hidden, memory, out_grad = hidden[0], memory[0], out_grad[0]

    packed, rows_own = pack_weights(
        info,
        query_weight.T,
        out_router.T,
        key_weight.T,
        value_router.T,
        value_weight.T,
        rel_weight.T,
        out_weight,
        memory,
        hidden,
    )
    ring_w = RingGather(packed, 1)
    ring_w.advance()
    rows_far, rows_pair = flip(rows_own, 2), flip(rows_own, 1)
    value_routes, out_routes, table = hold(
        value_routes, out_routes, sinusoid_reversed(key_count, width), packed
    )[:-1]
    codes = route_codes(
        value_routes[0].transpose(0, 2, 3, 1), out_routes[0].transpose(1, 2, 0), valid_mask
    )
    codes, rows_pair = ring_w.arrived(codes, rows_pair)
    ring_w.advance()
    codes_far = flip(codes, 2)
    codes_pair = flip(codes, 1)
    a_near = first_norm([rows_own, rows_pair], norm_gain, norm_bias, "first_norm_near")
    a_near, rows_far = ring_w.arrived(a_near, rows_far)
    ring_w.advance()
    rows_last = flip(rows_far, 1)
    a_far = first_norm([rows_far, rows_last], norm_gain, norm_bias, "first_norm_far")
    codes_last = flip(codes_far, 1)
    packed_ff = jnp.concatenate([up_weight, down_weight], axis=1)
    pick_v, pick_o = route_lanes(
        info, [codes, codes_pair, codes_far, codes_last], heads, head_width
    )
    a_far, packed_ff, pick_v, pick_o = ring_w.arrived(a_far, packed_ff, pick_v, pick_o)
    ring_w.advance()

    packed_ff, out_grad_sent = ring_w.arrived_last(packed_ff, out_grad)
    ring_f = RingGather(packed_ff, 0)
    ring_f.advance()
    grad_far = flip(out_grad_sent, 2)
    w_all, a_all, keys, values, vgate, expert, qu, qv, ogate, rel = project(
        ring_w, info, a_near, a_far, table, pick_v, pick_o, position_bias, window
    )
    qu, grad_far = ring_f.arrived(qu, grad_far)
    ring_f.advance()
    grad_parts = [out_grad, flip(out_grad_sent, 1), grad_far, flip(grad_far, 1)]
    probs, att = attention_forward(
        plan, slots, scale * math.log2(math.e), qu, qv, keys, values, rel
    )
    att, probs = ring_f.arrived(att, probs)
    ring_f.advance()
    mixed_pair, pair = out_projection(
        (1, 3), info, own, w_all, att, ogate, head_width, "out_projection_pair"
    )
    pair_in = flip(pair, 1)
    att, pair = hold(att, pair)
    mixed_own, near_far = out_projection(
        (0, 2), info, own, w_all, att, ogate, head_width, "out_projection_own"
    )
    pair_in, near_far = hold(pair_in, near_far)
    far_in = flip(add_far(near_far, 1, pair_in, 1), 2)
    (near_far,) = ring_f.arrived(near_far)
    ring_f.advance()
    middle, a_two, branch_sums = second_norm(
        hidden, near_far, pair_in, far_in, norm_gain, norm_bias, valid_mask
    )
    a_two_pair = flip(a_two, 1)
    a_two_far = flip(a_two, 2)
    (a_two_pair,) = ring_f.arrived_last(a_two_pair)

    d_near, d_pair, inner_near, dpre_near, w_ff = feed_forward(
        ring_f, None, [a_two, a_two_pair], grad_parts[:2], "feed_forward_near"
    )
    a_two_far, d_near, d_pair = hold(a_two_far, d_near, d_pair)
    d_pair = flip(d_pair, 1)
    a_parts = [a_two, a_two_pair, a_two_far, flip(a_two_far, 1)]
    d_far, d_last, inner_far, dpre_far = feed_forward(
        None, w_ff, a_parts[2:], grad_parts[2:], "feed_forward_far"
    )
    d_far_in = flip(add_far(d_far, None, flip(d_last, 1), None), 2)
    ff_blocks, ff_far = feed_forward_grads(
        a_parts, grad_parts, [inner_near, inner_far], [dpre_near, dpre_far]
    )
    y_near, y_pair, y_far, y_last = feed_forward_result(w_ff, [inner_near, inner_far], own)
    ring_g = RingSum([ff_blocks], *ff_far, 0)
    d_far_in, d_pair, y_near = ring_g.arrived(d_far_in, d_pair, y_near)
    d_mid, d_branch, sums_two = second_norm_back(
        middle, d_near, d_pair, d_far_in, out_grad, norm_gain
    )
    branch_far = flip(d_branch, 2)
    branch_pair = flip(d_branch, 1)
    ring_g.advance()

    branch_pair, y_pair, y_last = hold(branch_pair, y_pair, y_last)
    grads_near = attended_grads(
        (0, 1), info, [d_branch, branch_pair], w_all, att, ogate, head_width, "attended_grads_near"
    )
    y_pair = flip(y_pair, 1)
    y_last = flip(y_last, 1)
    scores_near = score_grads_near(
        info, slots, scale, head_width, probs, *grads_near, att, qu, qv, keys, values, rel
    )
    branch_far, near_a, near_b, y_last, near_query = ring_g.arrived(
        branch_far, *grads_near, y_last, scores_near[0]
    )
    ring_g.advance()
    branch_parts = [d_branch, branch_pair, branch_far, flip(branch_far, 1)]
    y_far_in = flip(add_far(y_far, None, y_last, None), 2)
    grads_far = attended_grads(
        (2, 3), info, branch_parts[2:], w_all, att, ogate, head_width, "attended_grads_far"
    )
    branch_all, d_att, d_ologit, d_expert, d_vlogit, mixed = value_grads(
        info,
        (near_a, near_b),
        grads_far,
        branch_parts,
        mixed_own,
        mixed_pair,
        probs,
        vgate,
        expert,
        plan,
        head_width,
    )
    experts = [(e * LANES, head_width) for e in range(EXPERTS)]
    kept = 2 * EXPERTS * head_width
    upper = tile_half(kept + 2 * LANES + head_width)
    value_blocks, (value_upper, value_lower) = column_grads(
        info,
        [(mixed, branch_all), (d_expert, a_all)],
        [experts, experts],
        part,
        upper,
        None,
        "out_and_value_grads",
    )
    d_att, value_blocks[0] = ring_g.arrived(d_att, value_blocks[0])
    ring_g.advance()
    d_query, d_key, d_rel, bias_sums = score_grads_far(
        info,
        slots,
        scale,
        head_width,
        (near_query,) + tuple(scores_near[1:]),
        probs,
        d_att,
        d_ologit,
        d_vlogit,
        att,
        qu,
        qv,
        keys,
        values,
        rel,
    )
    d_query, d_key, d_rel, y_far_in = hold(d_query, d_key, d_rel, y_far_in)
    late_blocks, late_far = column_grads(
        info,
        [(d_query, a_all), (d_key, a_all), (d_rel, table)],
        [[(0, LANES)], [(0, LANES)], [(0, head_width)]],
        part,
        None,
        value_lower,
        "query_key_rel_grads",
    )
    d_query, d_key, late_far[0] = hold(d_query, d_key, late_far[0])
    ring_v = RingSum([value_blocks, late_blocks], value_upper, late_far[0], 1)
    sums_c = input_grads(
        (0, 1, 2, 3), info, a_all, w_all, None, d_key, d_expert, "memory_sums"
    )[0]
    out_hidden, result_sums = final_result(middle, y_near, y_pair, y_far_in, valid_mask)
    pair, sums_a = input_grads(
        (1, 3), info, a_all, w_all, d_query, d_key, d_expert, "input_grads_pair"
    )
    d_query, sums_c, result_sums, pair = ring_g.arrived(
        *ring_v.arrived(d_query, sums_c, result_sums, pair)
    )
    ring_v.advance()
    pair_in = flip(pair, 1)
    far_near, sums_b = input_grads(
        (2, 0), info, a_all, w_all, d_query, d_key, d_expert, "input_grads_own"
    )
    far_in = add_far(far_near, 0, pair_in, 1)
    small = small_sums(
        info, sums_a, sums_b, sums_c, sums_two, bias_sums, branch_sums, result_sums, heads
    )
    small = small + flip(small, 1)
    small = small + flip(small, 2)
    small, far_in = hold(small, far_in)
    far_in = flip(far_in, 2)
    up_grad, down_grad = ring_g.finish(
        [(0, 0, part, 0, width), (0, 0, part, width, width)], "up_and_down_sum"
    )
    bit = 1
    while bit < lax.axis_size("dp"):
        small = sum_over_dp(small, bit)
        bit *= 2
        if bit in (2, 4):
            small, up_grad = ring_v.arrived(small, up_grad)
            ring_v.advance()
    smalls = [small]
    in_grad = first_norm_back(hidden, far_near, pair_in, far_in, d_mid, norm_gain)
    gain_grad, bias_grad, position_grad, stats = small_outputs(
        info, smalls, norm_gain, norm_bias, heads, head_width
    )
    in_grad, gain_grad, up_grad = ring_v.arrived(in_grad, gain_grad, up_grad)
    end = LANES + head_width
    out_weight_grad, value_grad, *late = ring_v.finish(
        [
            (0, 0, kept // 2, 0, part),
            (0, kept // 2, kept // 2, 0, part),
            (1, 0, head_width, 0, part),
            (1, head_width, EXPERTS, 0, part),
            (1, LANES, head_width, 0, part),
            (1, end, EXPERTS, 0, part),
            (1, 2 * LANES, head_width, 0, part),
        ],
        "weight_sums",
    )
    return (
        out_hidden[None],
        in_grad[None],
        gain_grad,
        bias_grad,
        late[0].T,
        late[2].T,
        late[4].T,
        value_grad.T,
        late[3].T,
        late[1].T,
        out_weight_grad,
        position_grad,
        up_grad,
        down_grad,
        stats[0, :2],
    )


def solution(mesh):
    return jax.shard_map(
        shards,
        mesh=mesh,
        in_specs=(
            P("dp", "head", None),
            P("dp", "head", None),
            P("dp", "head", None),
            P("dp", "head"),
            P("dp"),
            P("dp", None, "head", None, None),
            P("dp", "head", None, None),
            P(),
            P(),
            P("dp", "head"),
            P("dp", "head"),
            P("dp", "head"),
            P("dp", "head"),
            P("dp", "head"),
            P("dp", "head"),
            P("head", "dp"),
            P(None, "head"),
            P(("dp", "head"), None),
            P(("dp", "head"), None),
        ),
        out_specs=(
            P("dp", "head", None),
            P("dp", "head", None),
            P(),
            P(),
            P("dp", "head"),
            P("dp", "head"),
            P("dp", "head"),
            P("dp", "head"),
            P("dp", "head"),
            P("dp", "head"),
            P("head", "dp"),
            P(),
            P(("dp", "head"), None),
            P(("dp", "head"), None),
            P(),
        ),
        check_vma=False,
    )
```
